32 devices in a mesh: section: 4 (over y, x), clip: 8 (over z, core).
Axes of the slice: x: 2, y: 2, z: 4, core: 2. Of those that a mesh axis runs over, the one named last changes fastest.
Arguments:
- iframe_act: bfloat16 [4, 32, 14, 14, 1024], P('section', 'clip'), may hold values from -18 to 18
- motion_act: bfloat16 [4, 32, 14, 14, 256], P('section', 'clip'), may hold values from -18 to 18
- iframe_grad: bfloat16 [4, 32, 14, 14, 1024], P('section', 'clip'), may hold values from -18 to 18
- motion_grad: bfloat16 [4, 32, 14, 14, 256], P('section', 'clip'), may hold values from -18 to 18
- segment_valid: int32 [4, 32], P(None, 'clip'), may hold values from 0 to 1, as said below
- reduce_weight: bfloat16 [1024, 256], replicated, may hold values from -0.1875 to 0.1875
- spatial_weight: bfloat16 [3, 3, 256, 256], replicated, may hold values from -0.125 to 0.125
- expand_weight: bfloat16 [256, 1024], replicated, may hold values from -0.375 to 0.375
- motion_first: bfloat16 [3, 3, 256, 256], replicated, may hold values from -0.125 to 0.125
- motion_second: bfloat16 [3, 3, 256, 256], replicated, may hold values from -0.125 to 0.125
- reduce_norm: float32 [2, 256], replicated, may hold values from 0.5 to 1.5
- spatial_norm: float32 [2, 256], replicated, may hold values from 0.5 to 1.5
- expand_norm: float32 [2, 1024], replicated, may hold values from 0.5 to 1.5
- first_norm: float32 [2, 256], replicated, may hold values from 0.5 to 1.5
- second_norm: float32 [2, 256], replicated, may hold values from 0.5 to 1.5
Outputs:
- iframe_out: bfloat16 [4, 32, 14, 14, 1024], P('section', 'clip')
- motion_out: bfloat16 [4, 32, 14, 14, 256], P('section', 'clip')
- iframe_back: bfloat16 [4, 32, 14, 14, 1024], P('section', 'clip')
- motion_back: bfloat16 [4, 32, 14, 14, 256], P('section', 'clip')
- grad_reduce: float32 [1024, 256], replicated
- grad_spatial: float32 [3, 3, 256, 256], replicated
- grad_expand: float32 [256, 1024], replicated
- grad_first: float32 [3, 3, 256, 256], replicated
- grad_second: float32 [3, 3, 256, 256], replicated
- grad_reduce_norm: float32 [2, 256], replicated
- grad_spatial_norm: float32 [2, 256], replicated
- grad_expand_norm: float32 [2, 1024], replicated
- grad_first_norm: float32 [2, 256], replicated
- grad_second_norm: float32 [2, 256], replicated
The draws below stay inside these ranges and needn't reach their ends.
Inputs may be any that keep to these rules, and one draw needn't show every extreme that they name: `segment_valid`: frame 0 of each clip of 4 frames is 1.
All inputs are finite; a program needn't handle non-finite values.
Results may differ from the reference program's by a relative error of at most 0.0088.
Values may be sent and summed in bfloat16 or wider, within the bound.
No kernel may reach another device: no remote copies, remote signals or barrier semaphores. Data moves between devices by JAX's collectives and lax.ppermute only.
A program may use at most 192 MiB of HBM per device.

```python
import jax
import jax.numpy as jnp
from jax import lax

C_IN = 1024
C_MID = 256
C_MV = 256
HEIGHT = 14
WIDTH = 14
FR_DEV = 4
MICRO = 4
FRAMES = 32


def frame_levels(key):
    jitter = jax.random.uniform(key, (MICRO, FRAMES), jnp.float32)
    clip_place = (jnp.arange(FRAMES) // FR_DEV).astype(jnp.float32)
    return jnp.exp(jnp.log(3.0) * (clip_place[None, :] + jitter) / (FRAMES // FR_DEV))


def textured(key, channels):
    subkeys = jax.random.split(key, 3)
    extent = (MICRO, FRAMES, HEIGHT, WIDTH, channels)
    normal_part = jnp.clip(jax.random.normal(subkeys[0], extent, jnp.float32), -6.0, 6.0)
    levels = frame_levels(subkeys[2])
    mixed = normal_part
    return (mixed * levels[:, :, None, None, None]).astype(jnp.bfloat16)


def draw_iframe_act(key, part):
    key = jax.random.fold_in(key, 11)
    return textured(key, C_IN)


def draw_motion_act(key, part):
    key = jax.random.fold_in(key, 12)
    return textured(key, C_MV)


def draw_iframe_grad(key, part):
    key = jax.random.fold_in(key, 13)
    return textured(key, C_IN)


def draw_motion_grad(key, part):
    key = jax.random.fold_in(key, 14)
    return textured(key, C_MV)


def draw_segment_valid(key, part):
    key = jax.random.fold_in(key, 17)
    rolled = jax.random.randint(key, (MICRO, FRAMES), 0, 4)
    clip_start = (jnp.arange(FRAMES) % FR_DEV == 0)[None, :]
    return jnp.where(clip_start | (rolled < 3), 1, 0).astype(jnp.int32)


def normal_values(own_key, shape, spread, bound, held_as=jnp.bfloat16):
    return jnp.clip(spread * jax.random.normal(own_key, shape, jnp.float32), -bound, bound).astype(held_as)


def setup_inputs(seed: int = 0) -> dict:
    key_of = jax.random.split(jax.random.key(seed), 16)
    return {
        "iframe_act": draw_iframe_act(jax.random.fold_in(key_of[15], 71), 0),
        "motion_act": draw_motion_act(jax.random.fold_in(key_of[15], 71), 0),
        "iframe_grad": draw_iframe_grad(jax.random.fold_in(key_of[15], 71), 0),
        "motion_grad": draw_motion_grad(jax.random.fold_in(key_of[15], 71), 0),
        "segment_valid": draw_segment_valid(jax.random.fold_in(key_of[15], 71), 0),
        "reduce_weight": normal_values(key_of[5], (C_IN, C_MID), C_IN ** -0.5, 0.1875),
        "spatial_weight": normal_values(key_of[6], (3, 3, C_MID, C_MID), (9 * C_MID) ** -0.5, 0.125),
        "expand_weight": normal_values(key_of[7], (C_MID, C_IN), C_MID ** -0.5, 0.375),
        "motion_first": normal_values(key_of[8], (3, 3, C_MV, C_MV), (9 * C_MV) ** -0.5, 0.125),
        "motion_second": normal_values(key_of[9], (3, 3, C_MV, C_MV), (9 * C_MV) ** -0.5, 0.125),
        "reduce_norm": jnp.clip(jax.random.uniform(key_of[10], (2, C_MID), jnp.float32, 0.5, 1.5), 0.5, 1.5),
        "spatial_norm": jnp.clip(jax.random.uniform(key_of[11], (2, C_MID), jnp.float32, 0.5, 1.5), 0.5, 1.5),
        "expand_norm": jnp.clip(jax.random.uniform(key_of[12], (2, C_IN), jnp.float32, 0.5, 1.5), 0.5, 1.5),
        "first_norm": jnp.clip(jax.random.uniform(key_of[13], (2, C_MV), jnp.float32, 0.5, 1.5), 0.5, 1.5),
        "second_norm": jnp.clip(jax.random.uniform(key_of[14], (2, C_MV), jnp.float32, 0.5, 1.5), 0.5, 1.5),
    }


EPS = 1e-05

@jax.custom_vjp
def low(v):
    return lax.optimization_barrier(v.astype(jnp.bfloat16)).astype(jnp.float32)

@jax.custom_vjp
def low_back(v):
    return v

def low_keep(v):
    return (low(v), None)

def low_pass(kept, grad):
    return (grad,)

def back_keep(v):
    return (v, None)

def back_low(kept, grad):
    return (low(grad),)
low.defvjp(low_keep, low_pass)
low_back.defvjp(back_keep, back_low)

def pointwise(picture, matrix):
    return jnp.einsum('mfhwc,cd->mfhwd', picture, matrix, precision=lax.Precision.HIGHEST)

def spatial_conv(picture, kernel):
    extent = picture.shape
    merged = picture.reshape((extent[0] * extent[1],) + extent[2:])
    result = lax.conv_general_dilated(merged, kernel, (1, 1), ((1, 1), (1, 1)), dimension_numbers=('NHWC', 'HWIO', 'NHWC'), precision=lax.Precision.HIGHEST)
    return result.reshape(extent[:2] + result.shape[1:])

def batch_norm(preact, keep, params):
    pixel_count = lax.optimization_barrier(jnp.sum(keep, axis=(1, 2, 3, 4), keepdims=True)) * (preact.shape[2] * preact.shape[3])
    mean_value = lax.optimization_barrier(jnp.sum(keep * preact, axis=(1, 2, 3), keepdims=True)) / pixel_count
    square = lax.optimization_barrier(jnp.sum(keep * preact * preact, axis=(1, 2, 3), keepdims=True)) / pixel_count
    scale = lax.rsqrt(square - mean_value * mean_value + EPS)
    return params[0] * ((preact - mean_value) * scale) + params[1]

def reference(iframe_act, motion_act, iframe_grad, motion_grad, segment_valid, reduce_weight, spatial_weight, expand_weight, motion_first, motion_second, reduce_norm, spatial_norm, expand_norm, first_norm, second_norm):
    keep = segment_valid.astype(jnp.float32)[:, :, None, None, None]

    def forward(frames, motion, w_reduce, w_spatial, w_expand, w_first, w_second, n_reduce, n_spatial, n_expand, n_first, n_second):
        reduce_pre = low_back(pointwise(frames, w_reduce))
        reduce_act = low_back(low(jax.nn.silu(batch_norm(reduce_pre, keep, n_reduce))))
        spatial_pre = low_back(spatial_conv(reduce_act, w_spatial))
        spatial_act = low_back(low(jax.nn.silu(batch_norm(spatial_pre, keep, n_spatial))))
        expand_pre = low_back(pointwise(spatial_act, w_expand))
        iframe_result = keep * jax.nn.silu(batch_norm(expand_pre, keep, n_expand) + frames) + (1.0 - keep) * frames
        first_pre = low_back(spatial_conv(motion, w_first))
        motion_mid = low_back(low(jax.nn.silu(batch_norm(first_pre, keep, n_first))))
        second_pre = low_back(spatial_conv(motion_mid, w_second))
        motion_result = keep * jax.nn.silu(batch_norm(second_pre, keep, n_second) + motion) + (1.0 - keep) * motion
        return (iframe_result, motion_result)
    primals = (iframe_act.astype(jnp.float32), motion_act.astype(jnp.float32), reduce_weight.astype(jnp.float32), spatial_weight.astype(jnp.float32), expand_weight.astype(jnp.float32), motion_first.astype(jnp.float32), motion_second.astype(jnp.float32), reduce_norm, spatial_norm, expand_norm, first_norm, second_norm)
    results, pullback = jax.vjp(forward, *primals)
    grads = pullback((iframe_grad.astype(jnp.float32), motion_grad.astype(jnp.float32)))
    return (results[0].astype(jnp.bfloat16), results[1].astype(jnp.bfloat16), grads[0].astype(jnp.bfloat16), grads[1].astype(jnp.bfloat16), grads[2], grads[3], grads[4], grads[5], grads[6], grads[7], grads[8], grads[9], grads[10], grads[11])
```

```python
import jax
import jax.numpy as jnp
from jax import lax
from jax.sharding import PartitionSpec as P

EPS = 1e-05


def factors(size):
    steps = []
    stride = 1
    while size % 2 == 0 and stride < 2 and size > 1:
        steps.append((stride, 2))
        stride *= 2
        size //= 2
    while size % 4 == 0:
        steps.append((stride, 4))
        stride *= 4
        size //= 4
    while size % 2 == 0:
        steps.append((stride, 2))
        stride *= 2
        size //= 2
    return steps, size


def swap(value, axis, mask):
    size = lax.axis_size(axis)
    return lax.ppermute(value, axis, [(i, i ^ mask) for i in range(size)])


def clip_sum(value):
    steps, rest = factors(lax.axis_size("clip"))
    if rest != 1:
        return lax.psum(value, "clip")
    for stride, radix in steps:
        parts = [swap(value, "clip", stride * k) for k in range(1, radix)]
        for part in parts:
            value = value + part
    return value


def section_sum(value):
    size = lax.axis_size("section")
    if size & (size - 1):
        return lax.psum(value, "section")
    parts = [swap(value, "section", k) for k in range(1, size)]
    for part in parts:
        value = value + part
    return value


def reduce_step(value, axis, stride, radix):
    rows = value.shape[0] // radix
    here = (lax.axis_index(axis) // stride) % radix
    chunks = value.reshape((radix, rows) + value.shape[1:])
    own = lax.dynamic_index_in_dim(chunks, here, 0, keepdims=False).astype(jnp.float32)
    parts = []
    for k in range(1, radix):
        away = lax.dynamic_index_in_dim(chunks, here ^ k, 0, keepdims=False)
        parts.append(swap(away, axis, stride * k))
    for part in parts:
        own = own + part.astype(jnp.float32)
    return own.astype(value.dtype)


def gather_step(value, axis, stride, radix):
    here = (lax.axis_index(axis) // stride) % radix
    out = jnp.zeros((radix,) + value.shape, value.dtype)
    out = lax.dynamic_update_index_in_dim(out, value, here, 0)
    for k in range(1, radix):
        out = lax.dynamic_update_index_in_dim(out, swap(value, axis, stride * k), here ^ k, 0)
    return out.reshape((radix * value.shape[0],) + value.shape[1:])


def grad_sum(value):
    clip_steps, clip_rest = factors(lax.axis_size("clip"))
    section_steps, section_rest = factors(lax.axis_size("section"))
    if clip_rest != 1 or section_rest != 1:
        return lax.psum(value, ("section", "clip"))
    if lax.axis_size("section") == 4:
        section_steps = [(1, 4)]
    order = [("clip",) + clip_steps[0]]
    order += [("section",) + step for step in section_steps]
    order += [("clip",) + step for step in clip_steps[1:]]
    short = value.astype(jnp.bfloat16)
    for axis, stride, radix in order:
        short = reduce_step(short, axis, stride, radix)
    for axis, stride, radix in reversed(order):
        short = gather_step(short, axis, stride, radix)
    return short


def sigmoid(u):
    return 0.5 + 0.5 * jnp.tanh(0.5 * u)


def silu(u):
    return u * sigmoid(u)


def slope(u):
    s = sigmoid(u)
    return s * (1.0 + u * (1.0 - s))


def conv3(picture, kernel):
    return lax.conv_general_dilated(
        picture,
        kernel,
        (1, 1),
        ((1, 1), (1, 1)),
        dimension_numbers=("NHWC", "HWIO", "NHWC"),
        preferred_element_type=jnp.float32,
    )


def conv3_back(upstream, kernel):
    return conv3(upstream, jnp.transpose(kernel[::-1, ::-1], (0, 1, 3, 2)))


def conv3_grad(picture, upstream):
    rows_in, cols_in = picture.shape[1:3]
    padded = jnp.pad(picture, ((0, 0), (1, 1), (1, 1), (0, 0)))
    taps = []
    for a in range(3):
        for b in range(3):
            window = padded[:, a : a + rows_in, b : b + cols_in]
            taps.append(
                jnp.einsum("fhwc,fhwd->cd", window, upstream, preferred_element_type=jnp.float32)
            )
    return jnp.stack(taps)


def pointwise(picture, matrix):
    return jnp.einsum("fhwc,cd->fhwd", picture, matrix, preferred_element_type=jnp.float32)


def pixels(value):
    return jnp.sum(value, axis=(0, 1, 2))


def per_device(
    iframe_act,
    motion_act,
    iframe_grad,
    motion_grad,
    segment_valid,
    reduce_weight,
    spatial_weight,
    expand_weight,
    motion_first,
    motion_second,
    reduce_norm,
    spatial_norm,
    expand_norm,
    first_norm,
    second_norm,
):
    frames, motion = iframe_act[0], motion_act[0]
    rows_in, cols_in = frames.shape[1:3]
    frames_full, motion_full = frames.astype(jnp.float32), motion.astype(jnp.float32)
    iframe_cot, motion_cot = iframe_grad[0].astype(jnp.float32), motion_grad[0].astype(jnp.float32)
    keep_rows = lax.dynamic_index_in_dim(
        segment_valid, lax.axis_index("section"), 0, keepdims=False
    ).astype(jnp.float32)
    keep = keep_rows[:, None, None, None]

    def sums_of(z):
        return [pixels(keep * z), pixels(keep * z * z)]

    def moments(total, square, count):
        mean = total / count
        return mean, lax.rsqrt(square / count - mean * mean + EPS)

    def pooled(parts):
        sizes = [part.shape[0] for part in parts]
        flat = jnp.concatenate(parts)
        width = 256 * 8
        short = (-flat.shape[0]) % width
        flat = jnp.concatenate([flat, jnp.zeros((short,), jnp.float32)])
        flat = clip_sum(flat.reshape(-1, 256)).reshape(-1)
        out = []
        at = 0
        for size in sizes:
            out.append(flat[at : at + size])
            at += size
        return out

    def back(norm, scale, up, hat, total, cross, count):
        return (norm[0] * scale * (up - keep * (total + hat * cross) / count)).astype(jnp.bfloat16)

    reduce_pre = pointwise(frames, reduce_weight)
    first_pre = conv3(motion, motion_first)
    count_here = jnp.sum(keep_rows) * (rows_in * cols_in)
    got = pooled(
        sums_of(reduce_pre) + sums_of(first_pre) + [jnp.full((256,), count_here, jnp.float32)]
    )
    count = got[4][0]
    reduce_mean, reduce_scale = moments(got[0], got[1], count)
    first_mean, first_scale = moments(got[2], got[3], count)
    reduce_hat = (reduce_pre - reduce_mean) * reduce_scale
    first_hat = (first_pre - first_mean) * first_scale
    reduce_u = reduce_norm[0] * reduce_hat + reduce_norm[1]
    first_u = first_norm[0] * first_hat + first_norm[1]
    reduce_act = silu(reduce_u).astype(jnp.bfloat16)
    motion_mid = silu(first_u).astype(jnp.bfloat16)

    spatial_pre = conv3(reduce_act, spatial_weight)
    second_pre = conv3(motion_mid, motion_second)
    got = pooled(sums_of(spatial_pre) + sums_of(second_pre))
    spatial_mean, spatial_scale = moments(got[0], got[1], count)
    second_mean, second_scale = moments(got[2], got[3], count)
    spatial_hat = (spatial_pre - spatial_mean) * spatial_scale
    second_hat = (second_pre - second_mean) * second_scale
    spatial_u = spatial_norm[0] * spatial_hat + spatial_norm[1]
    spatial_act = silu(spatial_u).astype(jnp.bfloat16)
    second_u = second_norm[0] * second_hat + second_norm[1] + motion_full
    motion_out = (keep * silu(second_u) + (1.0 - keep) * motion_full).astype(jnp.bfloat16)
    second_up = motion_cot * keep * slope(second_u)

    expand_pre = pointwise(spatial_act, expand_weight)
    got = pooled(
        sums_of(expand_pre) + [pixels(second_up), pixels(second_up * second_hat)]
    )
    second_sums = got[2:]
    expand_mean, expand_scale = moments(got[0], got[1], count)
    second_back = back(second_norm, second_scale, second_up, second_hat, got[2], got[3], count)
    expand_hat = (expand_pre - expand_mean) * expand_scale
    expand_u = expand_norm[0] * expand_hat + expand_norm[1] + frames_full
    iframe_out = (keep * silu(expand_u) + (1.0 - keep) * frames_full).astype(jnp.bfloat16)
    expand_up = iframe_cot * keep * slope(expand_u)

    mid_grad = conv3_back(second_back, motion_second).astype(jnp.bfloat16)
    grad_second = conv3_grad(motion_mid, second_back)
    first_up = mid_grad.astype(jnp.float32) * slope(first_u)
    expand_sums = [pixels(expand_up), pixels(expand_up * expand_hat)]
    first_sums = [pixels(first_up), pixels(first_up * first_hat)]
    got = pooled(expand_sums + first_sums)
    expand_sums, first_sums = got[:2], got[2:]
    expand_back = back(expand_norm, expand_scale, expand_up, expand_hat, got[0], got[1], count)
    first_back = back(first_norm, first_scale, first_up, first_hat, got[2], got[3], count)
    motion_back = (
        motion_cot * (1.0 - keep) + second_up + conv3_back(first_back, motion_first)
    ).astype(jnp.bfloat16)
    grad_first = conv3_grad(motion, first_back)

    spatial_grad = jnp.einsum(
        "fhwd,cd->fhwc", expand_back, expand_weight, preferred_element_type=jnp.float32
    ).astype(jnp.bfloat16)
    grad_expand = jnp.einsum(
        "fhwc,fhwd->cd", spatial_act, expand_back, preferred_element_type=jnp.float32
    )
    spatial_up = spatial_grad.astype(jnp.float32) * slope(spatial_u)
    spatial_sums = [pixels(spatial_up), pixels(spatial_up * spatial_hat)]
    got = spatial_sums = pooled(spatial_sums)
    spatial_back = back(spatial_norm, spatial_scale, spatial_up, spatial_hat, got[0], got[1], count)

    reduce_grad = conv3_back(spatial_back, spatial_weight).astype(jnp.bfloat16)
    grad_spatial = conv3_grad(reduce_act, spatial_back)
    reduce_up = reduce_grad.astype(jnp.float32) * slope(reduce_u)
    reduce_sums = [pixels(reduce_up), pixels(reduce_up * reduce_hat)]
    got = reduce_sums = pooled(reduce_sums)
    reduce_back = back(reduce_norm, reduce_scale, reduce_up, reduce_hat, got[0], got[1], count)
    iframe_back = (
        iframe_cot * (1.0 - keep)
        + expand_up
        + jnp.einsum("fhwd,cd->fhwc", reduce_back, reduce_weight, preferred_element_type=jnp.float32)
    ).astype(jnp.bfloat16)
    grad_reduce = jnp.einsum(
        "fhwc,fhwd->cd", frames, reduce_back, preferred_element_type=jnp.float32
    )

    pieces = [grad_reduce, grad_spatial, grad_expand, grad_first, grad_second]
    flat = jnp.concatenate([piece.reshape(-1, 256) for piece in pieces])
    flat = grad_sum(flat).astype(jnp.float32)
    outs = []
    at = 0
    for weight in (reduce_weight, spatial_weight, expand_weight, motion_first, motion_second):
        size = weight.size // 256
        outs.append(flat[at : at + size].reshape(weight.shape))
        at += size
    flat = jnp.concatenate(
        [
            part
            for sums in (reduce_sums, spatial_sums, expand_sums, first_sums, second_sums)
            for part in (sums[1], sums[0])
        ]
    ).reshape(-1, 256)
    flat = section_sum(flat).reshape(-1)
    at = 0
    for norm in (reduce_norm, spatial_norm, expand_norm, first_norm, second_norm):
        outs.append(flat[at : at + norm.size].reshape(norm.shape))
        at += norm.size
    return (iframe_out[None], motion_out[None], iframe_back[None], motion_back[None]) + tuple(outs)


def solution(mesh):
    shared = (P("section", "clip", None, None, None),) * 4
    return jax.shard_map(
        per_device,
        mesh=mesh,
        in_specs=shared + (P(None, "clip"),) + (P(),) * 10,
        out_specs=shared + (P(),) * 10,
        check_vma=False,
    )
```

```python
import functools

import jax
import jax.numpy as jnp
from jax import lax
from jax.experimental import pallas as pl
from jax.experimental.pallas import tpu as pltpu
from jax.sharding import PartitionSpec as P

EPS = 1e-05
LANES = 128
F32 = jnp.float32
BF16 = jnp.bfloat16


def factors(size):
    steps = []
    stride = 1
    if size % 2 == 0:
        steps.append((stride, 2))
        stride, size = 2, size // 2
    while size % 4 == 0:
        steps.append((stride, 4))
        stride, size = stride * 4, size // 4
    while size % 2 == 0:
        steps.append((stride, 2))
        stride, size = stride * 2, size // 2
    return steps, size


def swap(value, axis, mask):
    size = lax.axis_size(axis)
    return lax.ppermute(value, axis, [(i, i ^ mask) for i in range(size)])


def clip_parts(value):
    steps, rest = factors(lax.axis_size("clip"))
    if rest != 1:
        return [lax.psum(value, "clip")]
    for stride, radix in steps[:-1]:
        parts = [swap(value, "clip", stride * k) for k in range(1, radix)]
        for part in parts:
            value = value + part
    stride, radix = steps[-1]
    return [value] + [swap(value, "clip", stride * k) for k in range(1, radix)]


def sigmoid(u):
    return 0.5 + 0.5 * jnp.tanh(0.5 * u)


def total_of(refs):
    total = refs[0][...]
    for ref in refs[1:]:
        total = total + ref[...]
    return total


def row_of(total, row, channels):
    count = channels // LANES
    return jnp.concatenate([total[row + k : row + k + 1] for k in range(count)], axis=1)


def put_row(ref, row, value):
    for k in range(value.shape[1] // LANES):
        ref[row + k : row + k + 1, :] = value[:, k * LANES : (k + 1) * LANES]


def moments(total, row, apart, channels, count):
    mean = row_of(total, row, channels) / count
    square = row_of(total, row + apart, channels) / count
    return mean, lax.rsqrt(square - mean * mean + EPS)


def eights(value):
    return value.reshape(-1, 8, value.shape[-1])


def rows_of(value):
    return value.reshape(-1, value.shape[-1])


def down(value):
    return jnp.sum(jnp.sum(value, axis=0), axis=0, keepdims=True)


def spread(value, width, frames, same_ref, edge_ref):
    rows, channels = value.shape
    line = width * frames
    index = lax.broadcasted_iota(jnp.int32, (line, channels), 0)
    first = jnp.where(index < frames, 0.0, 1.0).astype(F32)
    final = jnp.where(index >= line - frames, 0.0, 1.0).astype(F32)
    before = pltpu.roll(value, frames, 0).reshape(-1, line, channels) * first
    after = pltpu.roll(value, rows - frames, 0).reshape(-1, line, channels) * final
    zeros = jnp.zeros((line, channels), F32)
    for k, part in enumerate((rows_of(before), value, rows_of(after))):
        lanes = slice(k * channels, (k + 1) * channels)
        same_ref[:, lanes] = part.astype(BF16)
        edge_ref[:, lanes] = jnp.concatenate([zeros, part, zeros], axis=0).astype(BF16)


def tap_rows(same_ref, edge_ref, a):
    rows = same_ref.shape[0]
    if a == 1:
        return same_ref[...]
    start = a * (edge_ref.shape[0] - rows) // 2
    return edge_ref[start : start + rows, :]


def conv_of(same_ref, edge_ref, kernel_ref):
    total = None
    for a in range(3):
        matrix = kernel_ref[a].reshape(-1, kernel_ref.shape[3])
        part = jnp.dot(tap_rows(same_ref, edge_ref, a), matrix, preferred_element_type=F32)
        total = part if total is None else total + part
    return total


def conv_back_of(same_ref, edge_ref, kernel_ref):
    total = None
    channels = kernel_ref.shape[3]
    for a in range(3):
        rows = tap_rows(same_ref, edge_ref, a)
        for b in range(3):
            part = lax.dot_general(
                rows[:, b * channels : (b + 1) * channels],
                kernel_ref[2 - a, 2 - b],
                (((1,), (1,)), ((), ())),
                preferred_element_type=F32,
            )
            total = part if total is None else total + part
    return total


def split_store(core, keep_ref, send_ref, row, value):
    half = value.shape[0] // 2
    low, high = value[:half].astype(BF16), value[half:].astype(BF16)
    keep_ref[row : row + half, :] = jnp.where(core == 0, low, high)
    send_ref[row : row + half, :] = jnp.where(core == 0, high, low)


def across(first, second):
    return lax.dot_general(first, second, (((0,), (0,)), ((), ())), preferred_element_type=F32)


def conv_grad_to(core, picture, same_ref, edge_ref, keep_ref, send_ref, row):
    channels = same_ref.shape[1] // 3
    half = picture.shape[1] // 2
    for a in range(3):
        product = across(picture, tap_rows(same_ref, edge_ref, a))
        for b in range(3):
            tap = 3 * (2 - a) + 2 - b
            part = product[:, b * channels : (b + 1) * channels]
            split_store(core, keep_ref, send_ref, row + tap * half, part)


def back_of(up, z, mean, scale, gain, total_up, total_cross, count, mask):
    share = total_cross * scale / count
    start = total_up / count - mean * share
    return rows_of((gain * scale) * (eights(up) - mask * (start + eights(z) * share)))


def slope_back(grad, z, mean, scale, norm, ups_ref):
    hat = (z - mean) * scale
    u = norm[0:1] * hat + norm[1:2]
    s = sigmoid(u)
    up = grad.astype(BF16).astype(F32) * (s + u * s * (1.0 - s))
    ups_ref[...] = up
    return down(eights(up)), down(eights(up * hat))


def kernel_1(width, valid_far, x_far, m_far, reduce_far, first_far, mask8, zr, z1, sums, *rest):
    same, edge, valid, x, m, reduce_w, first_w, arrived = rest
    copies = []
    for k, (far, near) in enumerate(
        ((m_far, m), (valid_far, valid), (first_far, first_w), (x_far, x), (reduce_far, reduce_w))
    ):
        copies.append(pltpu.make_async_copy(far, near, arrived.at[k]))
        copies[k].start()
    channels = z1.shape[1]
    frames = m.shape[1]
    copies[0].wait()
    spread(rows_of(m[...]).astype(F32), width, frames, same, edge)
    copies[1].wait()
    section = lax.axis_index("section")
    keep = [valid[section, f].astype(F32) for f in range(frames)]
    frame = lax.rem(lax.broadcasted_iota(jnp.int32, (8, channels), 0), frames)
    mask = jnp.full((8, channels), 0.0, F32)
    for f in range(frames):
        mask = jnp.where(frame == f, keep[f], mask)
    mask8[...] = mask
    copies[2].wait()
    z1[...] = conv_of(same, edge, first_w)
    copies[3].wait()
    copies[4].wait()
    zr[...] = jnp.dot(rows_of(x[...]), reduce_w[...], preferred_element_type=F32)
    step = channels // LANES
    sums[...] = jnp.zeros(sums.shape, F32)
    for k, ref in enumerate((zr, z1)):
        z = eights(ref[...])
        kept = mask * z
        put_row(sums, 2 * k * step, down(kept))
        put_row(sums, (2 * k + 1) * step, down(kept * z))
    put_row(sums, 4 * step, jnp.full((1, LANES), 1.0, F32) * (sum(keep) * x.shape[0]))


def kernel_2(place, parts, mask8, zr, z1, reduce_n, first_n, spatial_w, second_w, *rest):
    total_1, ra, mm, zs, z2, sums, same, edge = rest
    channels = zr.shape[1]
    step = channels // LANES
    total = total_of(parts)
    total_1[...] = total
    count = total[4 * step : 4 * step + 1, 0:1]
    mask = mask8[...]
    for k, (z_ref, norm, act, weight, out) in enumerate(
        ((zr, reduce_n, ra, spatial_w, zs), (z1, first_n, mm, second_w, z2))
    ):
        mean, scale = moments(total, 2 * k * step, step, channels, count)
        gain = norm[0:1] * scale
        u = z_ref[...] * gain + (norm[1:2] - mean * gain)
        value = u * sigmoid(u)
        act[...] = value.astype(BF16)
        spread(value, *place, same, edge)
        out[...] = conv_of(same, edge, weight)
        z = eights(out[...])
        kept = mask * z
        put_row(sums, 2 * k * step, down(kept))
        put_row(sums, (2 * k + 1) * step, down(kept * z))


def kernel_3(parts, mask8, total_1, zs, z2, m, gm, spatial_n, second_n, expand_w, *rest):
    total_2, sa, ze, motion_out, up2, sums = rest
    channels, wide = zs.shape[1], ze.shape[1]
    step, wide_step = channels // LANES, wide // LANES
    total = total_of(parts)
    total_2[...] = total
    count = total_1[4 * step : 4 * step + 1, 0:1]
    mean, scale = moments(total, 0, step, channels, count)
    gain = spatial_n[0:1] * scale
    u = zs[...] * gain + (spatial_n[1:2] - mean * gain)
    sa[...] = (u * sigmoid(u)).astype(BF16)
    mask = mask8[...]
    sums[...] = jnp.zeros(sums.shape, F32)
    for at in range(0, wide, channels):
        lanes = slice(at, at + channels)
        ze[:, lanes] = jnp.dot(sa[...], expand_w[:, lanes], preferred_element_type=F32)
        z = eights(ze[:, lanes])
        kept = z * mask
        put_row(sums, at // LANES, down(kept))
        put_row(sums, wide_step + at // LANES, down(kept * z))
    mean, scale = moments(total, 2 * step, step, channels, count)
    hat = eights((z2[...] - mean) * scale)
    motion = eights(rows_of(m[...]).astype(F32))
    u = second_n[0:1] * hat + second_n[1:2] + motion
    s = sigmoid(u)
    w = u * s
    out = mask * w + (1.0 - mask) * motion
    motion_out[...] = rows_of(out).astype(BF16).reshape(motion_out.shape)
    up = eights(rows_of(gm[...]).astype(F32)) * mask * (s + w * (1.0 - s))
    up2[...] = rows_of(up)
    put_row(sums, 2 * wide_step, down(up))
    put_row(sums, 2 * wide_step + step, down(up * hat))


def kernel_4(place, parts, mask8, total_1, total_2, z1, z2, up2, ze, x, gx, *rest):
    expand_n, second_n, first_n, second_w = rest[:4]
    total_3, iframe_out, upe, up1, same, edge, sums = rest[4:]
    channels, wide = z1.shape[1], ze.shape[1]
    step, wide_step = channels // LANES, wide // LANES
    total = total_of(parts)
    total_3[...] = total
    count = total_1[4 * step : 4 * step + 1, 0:1]
    mask = mask8[...]

    mean, scale = moments(total_2[...], 2 * step, step, channels, count)
    low = back_of(
        up2[...], z2[...], mean, scale, second_n[0:1], row_of(total, 2 * wide_step, channels),
        row_of(total, 2 * wide_step + step, channels), count, mask,
    )
    spread(low.astype(BF16).astype(F32), *place, same, edge)
    mid_grad = conv_back_of(same, edge, second_w)
    mean, scale = moments(total_1[...], 2 * step, step, channels, count)
    total_up, total_cross = slope_back(mid_grad, z1[...], mean, scale, first_n, up1)
    sums[...] = jnp.zeros(sums.shape, F32)
    put_row(sums, 2 * wide_step, total_up)
    put_row(sums, 2 * wide_step + step, total_cross)

    part, rows = channels, 16
    frames = place[1]
    eight = (8, part)
    for at in range(0, wide, part):
        lanes = slice(at, at + part)
        mean, scale = moments(total, at // LANES, wide_step, part, count)
        mean8, scale8 = jnp.broadcast_to(mean, eight), jnp.broadcast_to(scale, eight)
        gain8 = jnp.broadcast_to(expand_n[0:1, lanes], eight)
        shift8 = jnp.broadcast_to(expand_n[1:2, lanes], eight)

        def step_of(i, totals):
            here = pl.ds(pl.multiple_of(i * rows, rows), rows)
            pixels = pl.ds(i * (rows // frames), rows // frames)
            hat = (eights(ze[here, lanes]) - mean8) * scale8
            x_here = eights(rows_of(x[pixels, :, lanes]).astype(F32))
            g_here = eights(rows_of(gx[pixels, :, lanes]).astype(F32))
            u = hat * gain8 + shift8 + x_here
            s = sigmoid(u)
            w = u * s
            out = mask * w + (1.0 - mask) * x_here
            iframe_out[pixels, :, lanes] = rows_of(out).astype(BF16).reshape(-1, frames, part)
            up = g_here * mask * (s + w * (1.0 - s))
            upe[here, lanes] = rows_of(up)
            cross = up * hat
            return (totals[0] + jnp.sum(up, axis=0), totals[1] + jnp.sum(cross, axis=0))

        empty = (jnp.zeros(eight, F32), jnp.zeros(eight, F32))
        totals = lax.fori_loop(0, ze.shape[0] // rows, step_of, empty, unroll=7)
        put_row(sums, at // LANES, down(totals[0][None]))
        put_row(sums, wide_step + at // LANES, down(totals[1][None]))


def kernel_5(parts, mask8, total_1, total_2, total_3, ze, upe, zs, expand_n, spatial_n, expand_w, *rest):
    total_4, back_e, ups, sums = rest
    channels, wide = zs.shape[1], ze.shape[1]
    step, wide_step = channels // LANES, wide // LANES
    total = total_of(parts)
    total_4[...] = total
    count = total_1[4 * step : 4 * step + 1, 0:1]
    mask = mask8[...]
    grad = None
    for at in range(0, wide, channels):
        lanes = slice(at, at + channels)
        mean, scale = moments(total_3[...], at // LANES, wide_step, channels, count)
        low = back_of(
            upe[:, lanes], ze[:, lanes], mean, scale, expand_n[0:1, lanes],
            row_of(total, at // LANES, channels), row_of(total, wide_step + at // LANES, channels),
            count, mask,
        )
        back_e[:, lanes] = low.astype(BF16)
        part = lax.dot_general(
            back_e[:, lanes], expand_w[:, lanes], (((1,), (1,)), ((), ())), preferred_element_type=F32
        )
        grad = part if grad is None else grad + part
    mean, scale = moments(total_2[...], 0, step, channels, count)
    total_up, total_cross = slope_back(grad, zs[...], mean, scale, spatial_n, ups)
    sums[...] = jnp.zeros(sums.shape, F32)
    put_row(sums, 0, total_up)
    put_row(sums, step, total_cross)


def kernel_6(place, parts, mask8, total_1, total_2, ups, zs, zr, spatial_n, reduce_n, spatial_w, *rest):
    total_5, upr, same, edge, sums = rest
    channels = zs.shape[1]
    step = channels // LANES
    total = total_of(parts)
    total_5[...] = total
    count = total_1[4 * step : 4 * step + 1, 0:1]
    mask = mask8[...]
    mean, scale = moments(total_2[...], 0, step, channels, count)
    low = back_of(
        ups[...], zs[...], mean, scale, spatial_n[0:1], row_of(total, 0, channels),
        row_of(total, step, channels), count, mask,
    )
    spread(low.astype(BF16).astype(F32), *place, same, edge)
    grad = conv_back_of(same, edge, spatial_w)
    mean, scale = moments(total_1[...], 0, step, channels, count)
    total_up, total_cross = slope_back(grad, zr[...], mean, scale, reduce_n, upr)
    sums[...] = jnp.zeros(sums.shape, F32)
    put_row(sums, 0, total_up)
    put_row(sums, step, total_cross)


def kernel_7(parts, mask8, total_1, upr, zr, reduce_n, back_r):
    channels = zr.shape[1]
    step = channels // LANES
    total = total_of(parts)
    count = total_1[4 * step : 4 * step + 1, 0:1]
    mask = mask8[...]
    mean, scale = moments(total_1[...], 0, step, channels, count)
    low = back_of(
        upr[...], zr[...], mean, scale, reduce_n[0:1], row_of(total, 0, channels),
        row_of(total, step, channels), count, mask,
    )
    back_r[...] = low.astype(BF16)


def kernel_motion(place, mask8, total_1, total_4, up1, z1, first_n, first_w, m, gm, up2, *rest):
    same_2, edge_2, mm, sa, back_e, motion_back, kept_ref, sent_ref, same, edge = rest
    channels = z1.shape[1]
    step, wide_step = channels // LANES, back_e.shape[1] // LANES
    count = total_1[4 * step : 4 * step + 1, 0:1]
    mask = mask8[...]
    mean, scale = moments(total_1[...], 2 * step, step, channels, count)
    total = total_4[...]
    low = back_of(
        up1[...], z1[...], mean, scale, first_n[0:1], row_of(total, 2 * wide_step, channels),
        row_of(total, 2 * wide_step + step, channels), count, mask,
    )
    spread(low.astype(BF16).astype(F32), *place, same, edge)
    out = conv_back_of(same, edge, first_w) + up2[...]
    out = rows_of(eights(out) + eights(rows_of(gm[...]).astype(F32)) * (1.0 - mask))
    motion_back[...] = out.astype(BF16).reshape(motion_back.shape)
    core = core_here()
    half = channels // 2
    conv_grad_to(core, mm[...], same_2, edge_2, kept_ref, sent_ref, 0)
    conv_grad_to(core, rows_of(m[...]), same, edge, kept_ref, sent_ref, 9 * half)
    for k in range(back_e.shape[1] // 256):
        product = across(sa[...], back_e[:, k * 256 : (k + 1) * 256])
        split_store(core, kept_ref, sent_ref, (18 + k) * half, product)


def kernel_last(ra, same, edge, x, back_r, sums_r, sums_s, sums_1, sums_2, kept_ref, sent_ref):
    core = core_here()
    channels, wide = ra.shape[1], x.shape[2]
    conv_grad_to(core, ra[...], same, edge, kept_ref, sent_ref, 0)
    product = across(rows_of(x[...]), back_r[...])
    at = 9 * (channels // 2)
    split_store(core, kept_ref, sent_ref, at, product)
    at = at + wide // 2
    rows = norm_rows(sums_r, 0, channels) + norm_rows(sums_s, 0, channels)
    rows += norm_rows(sums_1, 0, wide) + norm_rows(sums_1, 2 * wide // LANES, channels)
    rows += norm_rows(sums_2, 2 * wide // LANES, channels)
    half = kept_ref.shape[0] - at
    rows.append(jnp.zeros((2 * half - len(rows), 256), F32))
    split_store(core, kept_ref, sent_ref, at, jnp.concatenate(rows, axis=0))


def norm_rows(sums, row, channels):
    count = channels // LANES
    starts = list(range(row + count, row + 2 * count, 2)) + list(range(row, row + count, 2))
    return [jnp.concatenate([sums[k : k + 1, :], sums[k + 1 : k + 2, :]], axis=1) for k in starts]


def kernel_iframe(mask8, gx, upe, back_r, reduce_w, iframe_back):
    wide, part = upe.shape[1], 256
    mask, frames = mask8[...], gx.shape[1]
    for at in range(0, wide, part):
        lanes = slice(at, at + part)
        out = upe[:, lanes] + lax.dot_general(
            back_r[...], reduce_w[lanes, :], (((1,), (1,)), ((), ())), preferred_element_type=F32
        )
        out = eights(out) + eights(rows_of(gx[:, :, lanes]).astype(F32)) * (1.0 - mask)
        iframe_back[:, :, lanes] = rows_of(out).astype(BF16).reshape(-1, frames, part)


def core_here():
    return lax.rem(lax.axis_index("clip"), 2)


def place_on(axis, stride, radix):
    return lax.rem(lax.axis_index(axis) // stride, radix)


def kernel_scatter(axis, stride, radix, *refs):
    here = place_on(axis, stride, radix)
    ins, outs = refs[:-radix], refs[-radix:]
    for k in range(radix):
        at = jnp.bitwise_xor(here, k)
        total = ins[0][at].astype(F32)
        for ref in ins[1:]:
            total = total + ref[at].astype(F32)
        outs[k][...] = total.astype(BF16)


def kernel_sum(*refs):
    total = refs[0][...].astype(F32)
    for ref in refs[1:-1]:
        total = total + ref[...].astype(F32)
    refs[-1][...] = total.astype(BF16)


def kernel_gather(axis, stride, radix, *refs):
    here = place_on(axis, stride, radix)
    for k in range(radix):
        refs[-1][jnp.bitwise_xor(here, k)] = refs[k][...]


def kernel_finish(kinds, own, other, *outs):
    core = core_here()
    at = 0

    def halves(ref, lanes, size, at):
        here = pl.ds(pl.multiple_of(core * size, size), size)
        there = pl.ds(pl.multiple_of((1 - core) * size, size), size)
        ref[here, lanes] = own[at : at + size, :].astype(F32)
        ref[there, lanes] = other[at : at + size, :].astype(F32)

    for kind, out in zip(kinds, outs):
        if kind == "taps":
            size = out.shape[1] // 2
            for k in range(out.shape[0]):
                halves(out.at[k], slice(None), size, at)
                at = at + size
        elif kind == "wide":
            size = out.shape[0] // 2
            for k in range(out.shape[1] // 256):
                halves(out, slice(k * 256, (k + 1) * 256), size, at)
                at = at + size
        else:
            mine, his = own[at : at + 16, :].astype(F32), other[at : at + 16, :].astype(F32)
            rows = jnp.where(core == 0, mine, his)
            start = kind
            count = out.shape[1] // 256
            for k in range(2):
                for j in range(count):
                    row = start + k * count + j
                    out[k : k + 1, j * 256 : (j + 1) * 256] = rows[row : row + 1]


def call(kernel, outs, *args, scratch=(), flops=1 << 20, lists=None, space=pltpu.VMEM):
    def body(*refs):
        if lists:
            return kernel(refs[:lists], *refs[lists:])
        return kernel(*refs)

    moved = sum(arg.size * arg.dtype.itemsize for arg in args)
    moved += sum(out.size * out.dtype.itemsize for out in outs)
    return pl.pallas_call(
        body,
        out_shape=outs,
        in_specs=[pl.BlockSpec(memory_space=space) for _ in args],
        out_specs=[pl.BlockSpec(memory_space=pltpu.VMEM) for _ in outs],
        scratch_shapes=list(scratch),
        compiler_params=pltpu.CompilerParams(vmem_limit_bytes=20 << 20),
        cost_estimate=pl.CostEstimate(flops=flops, bytes_accessed=moved, transcendentals=0),
    )(*args)


def like(shape, dtype):
    return jax.ShapeDtypeStruct(shape, dtype)


def grad_sum(kept, sent, kinds, outs):
    clip_steps, clip_rest = factors(lax.axis_size("clip"))
    section = lax.axis_size("section")
    got = swap(sent, "clip", 1)
    rows, width = kept.shape
    order = [("section", 1, section)] + [("clip",) + step for step in clip_steps[1:]]
    ins = [kept, got]
    for axis, stride, radix in order:
        rows = rows // radix
        chunks = call(
            functools.partial(kernel_scatter, axis, stride, radix),
            [like((rows, width), BF16)] * radix,
            *[part.reshape(radix, rows, width) for part in ins],
        )
        ins = [chunks[0]] + [swap(chunks[k], axis, stride * k) for k in range(1, radix)]
    (value,) = call(kernel_sum, [like((rows, width), BF16)], *ins)
    for axis, stride, radix in reversed(order):
        parts = [value] + [swap(value, axis, stride * k) for k in range(1, radix)]
        (value,) = call(
            functools.partial(kernel_gather, axis, stride, radix),
            [like((radix,) + value.shape, BF16)],
            *parts,
        )
        value = value.reshape(-1, width)
    return call(functools.partial(kernel_finish, kinds), outs, value, swap(value, "clip", 1))


def per_device(
    iframe_act,
    motion_act,
    iframe_grad,
    motion_grad,
    segment_valid,
    reduce_weight,
    spatial_weight,
    expand_weight,
    motion_first,
    motion_second,
    reduce_norm,
    spatial_norm,
    expand_norm,
    first_norm,
    second_norm,
):
    frames, height, width, wide = iframe_act.shape[1:]
    narrow = motion_act.shape[4]

    def pixels_first(value):
        return jnp.transpose(value[0], (1, 2, 0, 3)).reshape(height * width, frames, value.shape[4])

    def frames_first(value):
        value = value.reshape(height, width, frames, value.shape[2])
        return jnp.transpose(value, (2, 0, 1, 3))[None]

    x, m, gx, gm = [pixels_first(v) for v in (iframe_act, motion_act, iframe_grad, motion_grad)]
    step, wide_step = narrow // LANES, wide // LANES
    area = height * width * frames

    def plane(channels, dtype=F32):
        return like((area, channels), dtype)

    def small(count):
        return like(((count + 7) // 8 * 8, LANES), F32)

    def bound(kernel):
        return functools.partial(kernel, (width, frames))

    def far(value):
        return pltpu.with_memory_space_constraint(value, pltpu.HBM)

    point = 2 * area * narrow * wide
    conv = 18 * area * narrow * narrow
    same = (area, 3 * narrow)
    edge = (area + 2 * width * frames, 3 * narrow)
    spread_scratch = [pltpu.VMEM(same, BF16), pltpu.VMEM(edge, BF16)]
    first_size, second_size = small(4 * step + 1), small(4 * step)
    both = small(2 * wide_step + 2 * step)

    mask8, zr, z1, sums = call(
        functools.partial(kernel_1, width),
        [like((8, narrow), F32), plane(narrow), plane(narrow), first_size],
        *[far(v) for v in (segment_valid, x, m, reduce_weight, motion_first)],
        scratch=spread_scratch
        + [pltpu.SMEM(segment_valid.shape, jnp.int32)]
        + [pltpu.VMEM(v.shape, BF16) for v in (x, m, reduce_weight, motion_first)]
        + [pltpu.SemaphoreType.DMA((5,))],
        flops=point + conv,
        space=pltpu.HBM,
    )
    parts = clip_parts(sums)
    total_1, ra, mm, zs, z2, sums = call(
        bound(kernel_2),
        [first_size, plane(narrow, BF16), plane(narrow, BF16), plane(narrow), plane(narrow), second_size],
        *parts, mask8, zr, z1, reduce_norm, first_norm, spatial_weight, motion_second,
        scratch=spread_scratch,
        flops=2 * conv,
        lists=len(parts),
    )
    parts = clip_parts(sums)
    total_2, sa, ze, motion_out, up2, sums = call(
        kernel_3,
        [second_size, plane(narrow, BF16), plane(wide), like(gm.shape, BF16), plane(narrow), both],
        *parts, mask8, total_1, zs, z2, m, gm, spatial_norm, second_norm, expand_weight,
        flops=point,
        lists=len(parts),
    )
    parts = clip_parts(sums)
    up2_sums = sums
    total_3, iframe_out, upe, up1, same_2, edge_2, sums = call(
        bound(kernel_4),
        [both, like(gx.shape, BF16), plane(wide), plane(narrow), like(same, BF16), like(edge, BF16), both],
        *parts, mask8, total_1, total_2, z1, z2, up2, ze, x, gx,
        expand_norm, second_norm, first_norm, motion_second,
        flops=conv,
        lists=len(parts),
    )
    parts = clip_parts(sums)
    up1_sums = sums
    total_4, back_e, ups, sums = call(
        kernel_5,
        [both, plane(wide, BF16), plane(narrow), small(2 * step)],
        *parts, mask8, total_1, total_2, total_3, ze, upe, zs, expand_norm, spatial_norm, expand_weight,
        flops=point,
        lists=len(parts),
    )
    parts = clip_parts(sums)
    ups_sums = sums
    half = narrow // 2
    set_rows = (18 + wide // 256) * half
    motion_back, kept, sent = call(
        bound(kernel_motion),
        [like(m.shape, BF16)] + [like((set_rows, 256), BF16)] * 2,
        mask8, total_1, total_4, up1, z1, first_norm, motion_first, m, gm, up2,
        same_2, edge_2, mm, sa, back_e,
        scratch=spread_scratch,
        flops=3 * conv + point,
    )
    taps = like((9, narrow, narrow), F32)
    grad_second, grad_first, grad_expand = grad_sum(
        kept, sent, ("taps", "taps", "wide"), [taps, taps, like(expand_weight.shape, F32)]
    )
    total_5, upr, same_s, edge_s, sums = call(
        bound(kernel_6),
        [small(2 * step), plane(narrow), like(same, BF16), like(edge, BF16), small(2 * step)],
        *parts, mask8, total_1, total_2, ups, zs, zr, spatial_norm, reduce_norm, spatial_weight,
        flops=conv,
        lists=len(parts),
    )
    parts = clip_parts(sums)
    upr_sums = sums
    (back_r,) = call(
        kernel_7,
        [plane(narrow, BF16)],
        *parts, mask8, total_1, upr, zr, reduce_norm,
        lists=len(parts),
    )

    spare = 128
    set_rows = 9 * half + wide // 2 + spare
    kept, sent = call(
        kernel_last,
        [like((set_rows, 256), BF16)] * 2,
        ra, same_s, edge_s, x, back_r, upr_sums, ups_sums, up1_sums, up2_sums,
        flops=conv + point,
    )
    (iframe_back,) = call(
        kernel_iframe, [like(gx.shape, BF16)], mask8, gx, upe, back_r, reduce_weight,
        flops=point,
    )
    norms = (reduce_norm, spatial_norm, expand_norm, first_norm, second_norm)
    starts = [0]
    for norm in norms:
        starts.append(starts[-1] + norm.size // 256)
    grad_spatial, grad_reduce, *norm_grads = grad_sum(
        kept, sent, ["taps", "taps"] + starts[:-1],
        [taps, like((1, wide, narrow), F32)] + [like(norm.shape, F32) for norm in norms],
    )
    features = tuple(frames_first(v) for v in (iframe_out, motion_out, iframe_back, motion_back))
    return features + (
        grad_reduce[0],
        grad_spatial.reshape(spatial_weight.shape),
        grad_expand,
        grad_first.reshape(motion_first.shape),
        grad_second.reshape(motion_second.shape),
    ) + tuple(norm_grads)


def solution(mesh):
    shared = (P("section", "clip", None, None, None),) * 4
    return jax.shard_map(
        per_device,
        mesh=mesh,
        in_specs=shared + (P(None, "clip"),) + (P(),) * 10,
        out_specs=shared + (P(),) * 10,
        check_vma=False,
    )
```

```python
import functools

import jax
import jax.numpy as jnp
from jax import lax
from jax.experimental import pallas as pl
from jax.experimental.pallas import tpu as pltpu
from jax.sharding import PartitionSpec as P

EPS = 1e-05
LANES = 128
COST = 1024
F32 = jnp.float32
BF16 = jnp.bfloat16


def factors(size):
    steps = []
    stride = 1
    if size % 2 == 0:
        steps.append((stride, 2))
        stride, size = 2, size // 2
    while size % 4 == 0:
        steps.append((stride, 4))
        stride, size = stride * 4, size // 4
    while size % 2 == 0:
        steps.append((stride, 2))
        stride, size = stride * 2, size // 2
    return steps, size


def swap(value, axis, mask):
    size = lax.axis_size(axis)
    return lax.ppermute(value, axis, [(i, i ^ mask) for i in range(size)])


def clip_parts(value):
    steps, rest = factors(lax.axis_size("clip"))
    if rest != 1:
        return [lax.psum(value, "clip")]
    for stride, radix in steps[:-1]:
        parts = [swap(value, "clip", stride * k) for k in range(1, radix)]
        for part in parts:
            value = value + part
    stride, radix = steps[-1]
    return [value] + [swap(value, "clip", stride * k) for k in range(1, radix)]


def sigmoid(u):
    return 0.5 + 0.5 * jnp.tanh(0.5 * u)


def total_of(refs):
    total = refs[0][...]
    for ref in refs[1:]:
        total = total + ref[...]
    return total


def row_of(total, row, channels):
    count = channels // LANES
    return jnp.concatenate([total[row + k : row + k + 1] for k in range(count)], axis=1)


def put_row(ref, row, value):
    for k in range(value.shape[1] // LANES):
        ref[row + k : row + k + 1, :] = value[:, k * LANES : (k + 1) * LANES]


def moments(total, row, apart, channels, count):
    mean = row_of(total, row, channels) / count
    square = row_of(total, row + apart, channels) / count
    return mean, lax.rsqrt(square - mean * mean + EPS)


def eights(value):
    return value.reshape(-1, 8, value.shape[-1])


def rows_of(value):
    return value.reshape(-1, value.shape[-1])


def down(value):
    return jnp.sum(jnp.sum(value, axis=0), axis=0, keepdims=True)


def spread(value, width, frames, same_ref, edge_ref):
    rows, channels = value.shape
    line = width * frames
    index = lax.broadcasted_iota(jnp.int32, (line, channels), 0)
    first = jnp.where(index < frames, 0.0, 1.0).astype(F32)
    final = jnp.where(index >= line - frames, 0.0, 1.0).astype(F32)
    before = pltpu.roll(value, frames, 0).reshape(-1, line, channels) * first
    after = pltpu.roll(value, rows - frames, 0).reshape(-1, line, channels) * final
    zeros = jnp.zeros((line, channels), F32)
    for k, part in enumerate((rows_of(before), value, rows_of(after))):
        lanes = slice(k * channels, (k + 1) * channels)
        same_ref[:, lanes] = part.astype(BF16)
        edge_ref[:, lanes] = jnp.concatenate([zeros, part, zeros], axis=0).astype(BF16)


def tap_rows(same_ref, edge_ref, a):
    rows = same_ref.shape[0]
    if a == 1:
        return same_ref[...]
    start = a * (edge_ref.shape[0] - rows) // 2
    return edge_ref[start : start + rows, :]


def conv_of(same_ref, edge_ref, kernel_ref):
    total = None
    for a in range(3):
        matrix = kernel_ref[a].reshape(-1, kernel_ref.shape[3])
        part = jnp.dot(tap_rows(same_ref, edge_ref, a), matrix, preferred_element_type=F32)
        total = part if total is None else total + part
    return total


def conv_back_of(same_ref, edge_ref, kernel_ref):
    total = None
    channels = kernel_ref.shape[3]
    for a in range(3):
        rows = tap_rows(same_ref, edge_ref, a)
        for b in range(3):
            part = lax.dot_general(
                rows[:, b * channels : (b + 1) * channels],
                kernel_ref[2 - a, 2 - b],
                (((1,), (1,)), ((), ())),
                preferred_element_type=F32,
            )
            total = part if total is None else total + part
    return total


def split_store(core, keep_ref, send_ref, row, value):
    half = value.shape[0] // 2
    low, high = value[:half].astype(BF16), value[half:].astype(BF16)
    keep_ref[row : row + half, :] = jnp.where(core == 0, low, high)
    send_ref[row : row + half, :] = jnp.where(core == 0, high, low)


def across(first, second):
    return lax.dot_general(first, second, (((0,), (0,)), ((), ())), preferred_element_type=F32)


def conv_grad_to(core, picture, same_ref, edge_ref, keep_ref, send_ref, row):
    channels = same_ref.shape[1] // 3
    half = picture.shape[1] // 2
    for a in range(3):
        product = across(picture, tap_rows(same_ref, edge_ref, a))
        for b in range(3):
            tap = 3 * (2 - a) + 2 - b
            part = product[:, b * channels : (b + 1) * channels]
            split_store(core, keep_ref, send_ref, row + tap * half, part)


def back_of(up, z, mean, scale, gain, total_up, total_cross, count, mask):
    share = total_cross * scale / count
    start = total_up / count - mean * share
    return rows_of((gain * scale) * (eights(up) - mask * (start + eights(z) * share)))


def slope_back(grad, z, mean, scale, norm, ups_ref):
    hat = (z - mean) * scale
    u = norm[0:1] * hat + norm[1:2]
    s = sigmoid(u)
    up = grad.astype(BF16).astype(F32) * (s + u * s * (1.0 - s))
    ups_ref[...] = up
    return down(eights(up)), down(eights(up * hat))


def kernel_1(width, valid_far, x_far, m_far, reduce_far, first_far, mask8, zr, z1, sums, *rest):
    same, edge, valid, x, m, reduce_w, first_w, arrived = rest
    copies = []
    for k, (far, near) in enumerate(
        ((m_far, m), (valid_far, valid), (first_far, first_w), (x_far, x), (reduce_far, reduce_w))
    ):
        copies.append(pltpu.make_async_copy(far, near, arrived.at[k]))
        copies[k].start()
    channels = z1.shape[1]
    frames = m.shape[1]
    copies[0].wait()
    spread(rows_of(m[...]).astype(F32), width, frames, same, edge)
    copies[1].wait()
    section = lax.axis_index("section")
    keep = [valid[section, f].astype(F32) for f in range(frames)]
    frame = lax.rem(lax.broadcasted_iota(jnp.int32, (8, channels), 0), frames)
    mask = jnp.full((8, channels), 0.0, F32)
    for f in range(frames):
        mask = jnp.where(frame == f, keep[f], mask)
    mask8[...] = mask
    copies[2].wait()
    z1[...] = conv_of(same, edge, first_w)
    copies[3].wait()
    copies[4].wait()
    zr[...] = jnp.dot(rows_of(x[...]), reduce_w[...], preferred_element_type=F32)
    step = channels // LANES
    sums[...] = jnp.zeros(sums.shape, F32)
    for k, ref in enumerate((zr, z1)):
        z = eights(ref[...])
        kept = mask * z
        put_row(sums, 2 * k * step, down(kept))
        put_row(sums, (2 * k + 1) * step, down(kept * z))
    put_row(sums, 4 * step, jnp.full((1, LANES), 1.0, F32) * (sum(keep) * x.shape[0]))


def kernel_2(place, parts, mask8, zr, z1, reduce_n, first_n, spatial_w, second_w, *rest):
    total_1, ra, mm, zs, z2, sums, same, edge = rest
    channels = zr.shape[1]
    step = channels // LANES
    total = total_of(parts)
    total_1[...] = total
    count = total[4 * step : 4 * step + 1, 0:1]
    mask = mask8[...]
    for k, (z_ref, norm, act, weight, out) in enumerate(
        ((zr, reduce_n, ra, spatial_w, zs), (z1, first_n, mm, second_w, z2))
    ):
        mean, scale = moments(total, 2 * k * step, step, channels, count)
        gain = norm[0:1] * scale
        u = z_ref[...] * gain + (norm[1:2] - mean * gain)
        value = u * sigmoid(u)
        act[...] = value.astype(BF16)
        spread(value, *place, same, edge)
        out[...] = conv_of(same, edge, weight)
        z = eights(out[...])
        kept = mask * z
        put_row(sums, 2 * k * step, down(kept))
        put_row(sums, (2 * k + 1) * step, down(kept * z))


def kernel_3(parts, mask8, total_1, zs, z2, m, gm, spatial_n, second_n, expand_w, *rest):
    total_2, sa, ze, up2, sums = rest
    channels, wide = zs.shape[1], ze.shape[1]
    step, wide_step = channels // LANES, wide // LANES
    total = total_of(parts)
    total_2[...] = total
    count = total_1[4 * step : 4 * step + 1, 0:1]
    mean, scale = moments(total, 0, step, channels, count)
    gain = spatial_n[0:1] * scale
    u = zs[...] * gain + (spatial_n[1:2] - mean * gain)
    sa[...] = (u * sigmoid(u)).astype(BF16)
    mask = mask8[...]
    sums[...] = jnp.zeros(sums.shape, F32)
    for at in range(0, wide, channels):
        lanes = slice(at, at + channels)
        ze[:, lanes] = jnp.dot(sa[...], expand_w[:, lanes], preferred_element_type=F32)
        z = eights(ze[:, lanes])
        kept = z * mask
        put_row(sums, at // LANES, down(kept))
        put_row(sums, wide_step + at // LANES, down(kept * z))
    mean, scale = moments(total, 2 * step, step, channels, count)
    hat = eights((z2[...] - mean) * scale)
    motion = eights(rows_of(m[...]).astype(F32))
    u = second_n[0:1] * hat + second_n[1:2] + motion
    s = sigmoid(u)
    up = eights(rows_of(gm[...]).astype(F32)) * mask * (s + u * s * (1.0 - s))
    up2[...] = rows_of(up)
    put_row(sums, 2 * wide_step, down(up))
    put_row(sums, 2 * wide_step + step, down(up * hat))


def kernel_4(place, parts, mask8, total_1, total_2, z1, z2, up2, ze, x, gx, *rest):
    expand_n, second_n, first_n, second_w = rest[:4]
    total_3, upe, up1, same, edge, sums = rest[4:]
    channels, wide = z1.shape[1], ze.shape[1]
    step, wide_step = channels // LANES, wide // LANES
    total = total_of(parts)
    total_3[...] = total
    count = total_1[4 * step : 4 * step + 1, 0:1]
    mask = mask8[...]

    mean, scale = moments(total_2[...], 2 * step, step, channels, count)
    low = back_of(
        up2[...], z2[...], mean, scale, second_n[0:1], row_of(total, 2 * wide_step, channels),
        row_of(total, 2 * wide_step + step, channels), count, mask,
    )
    spread(low.astype(BF16).astype(F32), *place, same, edge)
    mid_grad = conv_back_of(same, edge, second_w)
    mean, scale = moments(total_1[...], 2 * step, step, channels, count)
    total_up, total_cross = slope_back(mid_grad, z1[...], mean, scale, first_n, up1)
    sums[...] = jnp.zeros(sums.shape, F32)
    put_row(sums, 2 * wide_step, total_up)
    put_row(sums, 2 * wide_step + step, total_cross)

    part, rows = channels, 16
    frames = place[1]
    eight = (8, part)
    for at in range(0, wide, part):
        lanes = slice(at, at + part)
        mean, scale = moments(total, at // LANES, wide_step, part, count)
        mean8, scale8 = jnp.broadcast_to(mean, eight), jnp.broadcast_to(scale, eight)
        gain8 = jnp.broadcast_to(expand_n[0:1, lanes], eight)
        shift8 = jnp.broadcast_to(expand_n[1:2, lanes], eight)

        def step_of(i, totals):
            here = pl.ds(pl.multiple_of(i * rows, rows), rows)
            pixels = pl.ds(i * (rows // frames), rows // frames)
            hat = (eights(ze[here, lanes]) - mean8) * scale8
            x_here = eights(rows_of(x[pixels, :, lanes]).astype(F32))
            g_here = eights(rows_of(gx[pixels, :, lanes]).astype(F32))
            u = hat * gain8 + shift8 + x_here
            s = sigmoid(u)
            up = g_here * mask * (s + u * s * (1.0 - s))
            upe[here, lanes] = rows_of(up)
            cross = up * hat
            return (totals[0] + jnp.sum(up, axis=0), totals[1] + jnp.sum(cross, axis=0))

        empty = (jnp.zeros(eight, F32), jnp.zeros(eight, F32))
        totals = lax.fori_loop(0, ze.shape[0] // rows, step_of, empty, unroll=7)
        put_row(sums, at // LANES, down(totals[0][None]))
        put_row(sums, wide_step + at // LANES, down(totals[1][None]))


def kernel_5(parts, mask8, total_1, total_2, total_3, ze, upe, zs, expand_n, spatial_n, expand_w, *rest):
    total_4, back_e, ups, sums = rest
    channels, wide = zs.shape[1], ze.shape[1]
    step, wide_step = channels // LANES, wide // LANES
    total = total_of(parts)
    total_4[...] = total
    count = total_1[4 * step : 4 * step + 1, 0:1]
    mask = mask8[...]
    grad = None
    for at in range(0, wide, channels):
        lanes = slice(at, at + channels)
        mean, scale = moments(total_3[...], at // LANES, wide_step, channels, count)
        low = back_of(
            upe[:, lanes], ze[:, lanes], mean, scale, expand_n[0:1, lanes],
            row_of(total, at // LANES, channels), row_of(total, wide_step + at // LANES, channels),
            count, mask,
        )
        back_e[:, lanes] = low.astype(BF16)
        part = lax.dot_general(
            back_e[:, lanes], expand_w[:, lanes], (((1,), (1,)), ((), ())), preferred_element_type=F32
        )
        grad = part if grad is None else grad + part
    mean, scale = moments(total_2[...], 0, step, channels, count)
    total_up, total_cross = slope_back(grad, zs[...], mean, scale, spatial_n, ups)
    sums[...] = jnp.zeros(sums.shape, F32)
    put_row(sums, 0, total_up)
    put_row(sums, step, total_cross)


def kernel_6(place, parts, mask8, total_1, total_2, ups, zs, zr, spatial_n, reduce_n, spatial_w, *rest):
    total_5, upr, same, edge, sums = rest
    channels = zs.shape[1]
    step = channels // LANES
    total = total_of(parts)
    total_5[...] = total
    count = total_1[4 * step : 4 * step + 1, 0:1]
    mask = mask8[...]
    mean, scale = moments(total_2[...], 0, step, channels, count)
    low = back_of(
        ups[...], zs[...], mean, scale, spatial_n[0:1], row_of(total, 0, channels),
        row_of(total, step, channels), count, mask,
    )
    spread(low.astype(BF16).astype(F32), *place, same, edge)
    grad = conv_back_of(same, edge, spatial_w)
    mean, scale = moments(total_1[...], 0, step, channels, count)
    total_up, total_cross = slope_back(grad, zr[...], mean, scale, reduce_n, upr)
    sums[...] = jnp.zeros(sums.shape, F32)
    put_row(sums, 0, total_up)
    put_row(sums, step, total_cross)


def kernel_second(mm, same, edge, kept_ref, sent_ref):
    conv_grad_to(core_here(), mm[...], same, edge, kept_ref, sent_ref, 0)


def kernel_first(place, mask8, total_1, total_4, up1, z1, first_n, m, sa, back_e, *rest):
    kept_in, sent_in, same, edge, kept_ref, sent_ref = rest
    channels = z1.shape[1]
    step, wide_step = channels // LANES, back_e.shape[1] // LANES
    count = total_1[4 * step : 4 * step + 1, 0:1]
    mean, scale = moments(total_1[...], 2 * step, step, channels, count)
    total = total_4[...]
    low = back_of(
        up1[...], z1[...], mean, scale, first_n[0:1], row_of(total, 2 * wide_step, channels),
        row_of(total, 2 * wide_step + step, channels), count, mask8[...],
    )
    spread(low.astype(BF16).astype(F32), *place, same, edge)
    core = core_here()
    half = channels // 2
    conv_grad_to(core, rows_of(m[...]), same, edge, kept_ref, sent_ref, 9 * half)
    for k in range(back_e.shape[1] // 256):
        product = across(sa[...], back_e[:, k * 256 : (k + 1) * 256])
        split_store(core, kept_ref, sent_ref, (18 + k) * half, product)


def kernel_motion(mask8, same, edge, first_w, gm, up2, motion_back):
    out = conv_back_of(same, edge, first_w) + up2[...]
    out = rows_of(eights(out) + eights(rows_of(gm[...]).astype(F32)) * (1.0 - mask8[...]))
    motion_back[...] = out.astype(BF16).reshape(motion_back.shape)


def kernel_spatial(ra, same, edge, kept_ref, sent_ref):
    conv_grad_to(core_here(), ra[...], same, edge, kept_ref, sent_ref, 0)


def kernel_7(parts, mask8, total_1, upr, zr, reduce_n, x, sums_r, sums_s, sums_1, sums_2, *rest):
    kept_in, sent_in, back_r, kept_ref, sent_ref = rest
    channels, wide = zr.shape[1], x.shape[2]
    step = channels // LANES
    total = total_of(parts)
    count = total_1[4 * step : 4 * step + 1, 0:1]
    mean, scale = moments(total_1[...], 0, step, channels, count)
    low = back_of(
        upr[...], zr[...], mean, scale, reduce_n[0:1], row_of(total, 0, channels),
        row_of(total, step, channels), count, mask8[...],
    )
    back_r[...] = low.astype(BF16)
    core = core_here()
    at = 9 * (channels // 2)
    split_store(core, kept_ref, sent_ref, at, across(rows_of(x[...]), back_r[...]))
    at = at + wide // 2
    rows = norm_rows(sums_r, 0, channels) + norm_rows(sums_s, 0, channels)
    rows += norm_rows(sums_1, 0, wide) + norm_rows(sums_1, 2 * wide // LANES, channels)
    rows += norm_rows(sums_2, 2 * wide // LANES, channels)
    half = kept_ref.shape[0] - at
    rows.append(jnp.zeros((2 * half - len(rows), 256), F32))
    split_store(core, kept_ref, sent_ref, at, jnp.concatenate(rows, axis=0))


def kernel_out(place, mask8, total_1, total_2, total_3, ze, x, z2, m, expand_n, second_n, iframe_out, motion_out):
    channels, wide = z2.shape[1], ze.shape[1]
    step, wide_step = channels // LANES, wide // LANES
    count = total_1[4 * step : 4 * step + 1, 0:1]
    mask = mask8[...]

    def joined(z, here, mean, scale, norm):
        u = eights(z) * (norm[0:1] * scale) + (norm[1:2] - mean * (norm[0:1] * scale)) + here
        return rows_of(mask * (u * sigmoid(u)) + (1.0 - mask) * here).astype(BF16)

    mean, scale = moments(total_2[...], 2 * step, step, channels, count)
    motion = eights(rows_of(m[...]).astype(F32))
    motion_out[...] = joined(z2[...], motion, mean, scale, second_n[...]).reshape(motion_out.shape)
    part, rows, frames = channels, 16, place[1]
    for at in range(0, wide, part):
        lanes = slice(at, at + part)
        mean, scale = moments(total_3[...], at // LANES, wide_step, part, count)
        norm = expand_n[:, lanes]

        def step_of(i, carry):
            here = pl.ds(pl.multiple_of(i * rows, rows), rows)
            pixels = pl.ds(i * (rows // frames), rows // frames)
            frame = eights(rows_of(x[pixels, :, lanes]).astype(F32))
            out = joined(ze[here, lanes], frame, mean, scale, norm)
            iframe_out[pixels, :, lanes] = out.reshape(-1, frames, part)
            return carry

        lax.fori_loop(0, ze.shape[0] // rows, step_of, 0, unroll=7)


def norm_rows(sums, row, channels):
    count = channels // LANES
    starts = list(range(row + count, row + 2 * count, 2)) + list(range(row, row + count, 2))
    return [jnp.concatenate([sums[k : k + 1, :], sums[k + 1 : k + 2, :]], axis=1) for k in starts]


def kernel_iframe(mask8, gx, upe, back_r, reduce_w, iframe_back):
    wide, part = upe.shape[1], 256
    mask, frames = mask8[...], gx.shape[1]
    for at in range(0, wide, part):
        lanes = slice(at, at + part)
        out = upe[:, lanes] + lax.dot_general(
            back_r[...], reduce_w[lanes, :], (((1,), (1,)), ((), ())), preferred_element_type=F32
        )
        out = eights(out) + eights(rows_of(gx[:, :, lanes]).astype(F32)) * (1.0 - mask)
        iframe_back[:, :, lanes] = rows_of(out).astype(BF16).reshape(-1, frames, part)


def core_here():
    return lax.rem(lax.axis_index("clip"), 2)


def kernel_scatter(phase, *refs):
    here, radix = phase.digit(), phase.radix
    ins, outs = refs[:-radix], refs[-radix:]
    for k in range(radix):
        at = jnp.bitwise_xor(here, k)
        total = ins[0][at].astype(F32)
        for ref in ins[1:]:
            total = total + ref[at].astype(F32)
        outs[k][...] = total.astype(BF16)


def kernel_sum(*refs):
    total = refs[0][...].astype(F32)
    for ref in refs[1:-1]:
        total = total + ref[...].astype(F32)
    refs[-1][...] = total.astype(BF16)


def kernel_gather(phase, *refs):
    here = phase.digit()
    for k in range(phase.radix):
        refs[-1][jnp.bitwise_xor(here, k)] = refs[k][...]


def kernel_finish(kinds, own, other, *outs):
    core = core_here()
    at = 0

    def halves(ref, lanes, size, at):
        here = pl.ds(pl.multiple_of(core * size, size), size)
        there = pl.ds(pl.multiple_of((1 - core) * size, size), size)
        ref[here, lanes] = own[at : at + size, :].astype(F32)
        ref[there, lanes] = other[at : at + size, :].astype(F32)

    for kind, out in zip(kinds, outs):
        if kind == "taps":
            size = out.shape[1] // 2
            for k in range(out.shape[0]):
                halves(out.at[k], slice(None), size, at)
                at = at + size
        elif kind == "wide":
            size = out.shape[0] // 2
            for k in range(out.shape[1] // 256):
                halves(out, slice(k * 256, (k + 1) * 256), size, at)
                at = at + size
        else:
            mine, his = own[at : at + 16, :].astype(F32), other[at : at + 16, :].astype(F32)
            rows = jnp.where(core == 0, mine, his)
            start = kind
            count = out.shape[1] // 256
            for k in range(2):
                for j in range(count):
                    row = start + k * count + j
                    out[k : k + 1, j * 256 : (j + 1) * 256] = rows[row : row + 1]


def call(kernel, outs, *args, scratch=(), lists=None, space=pltpu.VMEM, after=(), alias=(), token=False):
    used = len(args)
    if token:
        outs = list(outs) + [like((8, LANES), F32)]

    def body(*refs):
        refs = refs[:used] + refs[used + len(after) :]
        if token:
            at = used + len(outs) - 1
            refs[at][...] = jnp.zeros((8, LANES), F32)
            refs = refs[:at] + refs[at + 1 :]
        if lists:
            return kernel(refs[:lists], *refs[lists:])
        return kernel(*refs)

    return pl.pallas_call(
        body,
        out_shape=outs,
        in_specs=[pl.BlockSpec(memory_space=space) for _ in args]
        + [pl.BlockSpec(memory_space=pl.ANY) for _ in after],
        out_specs=[pl.BlockSpec(memory_space=pltpu.VMEM) for _ in outs],
        scratch_shapes=list(scratch),
        input_output_aliases=dict(alias),
        compiler_params=pltpu.CompilerParams(vmem_limit_bytes=20 << 20),
        cost_estimate=pl.CostEstimate(flops=COST, bytes_accessed=COST, transcendentals=0),
    )(*args, *after)


def like(shape, dtype):
    return jax.ShapeDtypeStruct(shape, dtype)


class Phase:
    def __init__(self, radix, digit, partner):
        self.radix, self.digit, self.partner = radix, digit, partner

    def send(self, value, k):
        sections, clips = lax.axis_size("section"), lax.axis_size("clip")
        route = []
        for s in range(sections):
            for c in range(clips):
                to, where = self.partner(s, c, k)
                route.append((s * clips + c, to * clips + where))
        return lax.ppermute(value, ("section", "clip"), route)


def over_section():
    size = lax.axis_size("section")
    return [Phase(size, lambda: lax.axis_index("section"), lambda s, c, k: (s ^ k, c))]


def over_section_halves():
    if lax.axis_size("section") != 4:
        return over_section()

    def digit(swapped):
        section = lax.axis_index("section")
        first = jnp.bitwise_xor(core_here(), swapped) == 0
        return jnp.where(first, lax.rem(section, 2), section // 2)

    def partner(swapped, s, c, k):
        return s ^ (k if (c % 2) ^ swapped == 0 else 2 * k), c

    return [
        Phase(2, functools.partial(digit, swapped), functools.partial(partner, swapped))
        for swapped in (0, 1)
    ]


def over_clip():
    def phase(stride, radix):
        return Phase(
            radix,
            lambda: lax.rem(lax.axis_index("clip") // stride, radix),
            lambda s, c, k: (s, c ^ (stride * k)),
        )

    return [phase(stride, radix) for stride, radix in factors(lax.axis_size("clip"))[0][1:]]


def over_clip_halves():
    def digit(stride, swapped):
        first = jnp.bitwise_xor(core_here(), swapped) == 0
        place = lax.axis_index("clip") // stride
        return jnp.where(first, lax.rem(place, 2), lax.rem(place // 2, 2))

    def partner(stride, swapped, s, c, k):
        return s, c ^ (stride * (k if (c % 2) ^ swapped == 0 else 2 * k))

    phases = []
    for step, (stride, radix) in zip(over_clip(), factors(lax.axis_size("clip"))[0][1:]):
        if radix != 4:
            phases.append(step)
            continue
        for swapped in (0, 1):
            phases.append(
                Phase(
                    2,
                    functools.partial(digit, stride, swapped),
                    functools.partial(partner, stride, swapped),
                )
            )
    return phases


class GradSum:
    def __init__(self, kept, sent, phases):
        self.phases = phases
        self.rows, self.width = kept.shape
        self.parts = [kept, swap(sent, "clip", 1)]

    def scatter(self, k, after=()):
        phase = self.phases[k]
        radix = phase.radix
        self.rows = self.rows // radix
        chunks = call(
            functools.partial(kernel_scatter, phase),
            [like((self.rows, self.width), BF16)] * radix,
            *[part.reshape(radix, self.rows, self.width) for part in self.parts],
            after=after,
        )
        self.parts = [chunks[0]] + [phase.send(chunks[j], j) for j in range(1, radix)]
        return chunks[0]

    def spread_from(self, value, k):
        phase = self.phases[k]
        self.parts = [value] + [phase.send(value, j) for j in range(1, phase.radix)]
        return value

    def total(self, after=()):
        (value,) = call(kernel_sum, [like((self.rows, self.width), BF16)], *self.parts, after=after)
        return self.spread_from(value, len(self.phases) - 1)

    def gather(self, k, after=()):
        radix = self.phases[k].radix
        (value,) = call(
            functools.partial(kernel_gather, self.phases[k]),
            [like((radix, self.rows, self.width), BF16)],
            *self.parts,
            after=after,
        )
        self.rows = radix * self.rows
        value = value.reshape(self.rows, self.width)
        if k:
            return self.spread_from(value, k - 1)
        self.parts = [value, swap(value, "clip", 1)]
        return value

    def finish(self, kinds, outs, token=False):
        return call(functools.partial(kernel_finish, kinds), outs, *self.parts, token=token)


FIRST_PHASES = (over_section_halves, over_clip)
SECOND_PHASES = (over_section, over_clip)
EARLY = 1
ORDER = ("Ts0", "I", "M", "Fs2", "O", "Ts1", "Ft", "Fg2", "Tt", "Fg1", "Tg1", "Fg0", "X", "Tg0")


def per_device(
    iframe_act,
    motion_act,
    iframe_grad,
    motion_grad,
    segment_valid,
    reduce_weight,
    spatial_weight,
    expand_weight,
    motion_first,
    motion_second,
    reduce_norm,
    spatial_norm,
    expand_norm,
    first_norm,
    second_norm,
):
    frames, height, width, wide = iframe_act.shape[1:]
    narrow = motion_act.shape[4]

    def pixels_first(value):
        return jnp.transpose(value[0], (1, 2, 0, 3)).reshape(height * width, frames, value.shape[4])

    def frames_first(value):
        value = value.reshape(height, width, frames, value.shape[2])
        return jnp.transpose(value, (2, 0, 1, 3))[None]

    x, m, gx, gm = [pixels_first(v) for v in (iframe_act, motion_act, iframe_grad, motion_grad)]
    step, wide_step = narrow // LANES, wide // LANES
    area = height * width * frames

    def plane(channels, dtype=F32):
        return like((area, channels), dtype)

    def small(count):
        return like(((count + 7) // 8 * 8, LANES), F32)

    def bound(kernel):
        return functools.partial(kernel, (width, frames))

    def far(value):
        return pltpu.with_memory_space_constraint(value, pltpu.HBM)

    same = (area, 3 * narrow)
    edge = (area + 2 * width * frames, 3 * narrow)
    spread_scratch = [pltpu.VMEM(same, BF16), pltpu.VMEM(edge, BF16)]
    first_size, second_size = small(4 * step + 1), small(4 * step)
    both = small(2 * wide_step + 2 * step)

    mask8, zr, z1, sums = call(
        functools.partial(kernel_1, width),
        [like((8, narrow), F32), plane(narrow), plane(narrow), first_size],
        *[far(v) for v in (segment_valid, x, m, reduce_weight, motion_first)],
        scratch=spread_scratch
        + [pltpu.SMEM(segment_valid.shape, jnp.int32)]
        + [pltpu.VMEM(v.shape, BF16) for v in (x, m, reduce_weight, motion_first)]
        + [pltpu.SemaphoreType.DMA((5,))],
        space=pltpu.HBM,
    )
    parts = clip_parts(sums)
    total_1, ra, mm, zs, z2, sums = call(
        bound(kernel_2),
        [first_size, plane(narrow, BF16), plane(narrow, BF16), plane(narrow), plane(narrow), second_size],
        *parts, mask8, zr, z1, reduce_norm, first_norm, spatial_weight, motion_second,
        scratch=spread_scratch,
        lists=len(parts),
    )
    parts = clip_parts(sums)
    total_2, sa, ze, up2, sums = call(
        kernel_3,
        [second_size, plane(narrow, BF16), plane(wide), plane(narrow), both],
        *parts, mask8, total_1, zs, z2, m, gm, spatial_norm, second_norm, expand_weight,
        lists=len(parts),
    )
    parts = clip_parts(sums)
    up2_sums = sums
    total_3, upe, up1, same_2, edge_2, sums = call(
        bound(kernel_4),
        [both, plane(wide), plane(narrow), like(same, BF16), like(edge, BF16), both],
        *parts, mask8, total_1, total_2, z1, z2, up2, ze, x, gx,
        expand_norm, second_norm, first_norm, motion_second,
        lists=len(parts),
    )
    parts = clip_parts(sums)
    up1_sums = sums
    half = narrow // 2
    set_rows = (18 + wide // 256) * half
    kept, sent = call(
        kernel_second,
        [like((set_rows, 256), BF16)] * 2,
        mm, same_2, edge_2,
        after=parts[:1],
    )
    total_4, back_e, ups, sums = call(
        kernel_5,
        [both, plane(wide, BF16), plane(narrow), small(2 * step)],
        *parts, mask8, total_1, total_2, total_3, ze, upe, zs, expand_norm, spatial_norm, expand_weight,
        lists=len(parts),
        after=[kept],
    )
    parts = clip_parts(sums)
    ups_sums = sums
    same_1, edge_1, kept, sent = call(
        bound(kernel_first),
        [like(same, BF16), like(edge, BF16)] + [like((set_rows, 256), BF16)] * 2,
        mask8, total_1, total_4, up1, z1, first_norm, m, sa, back_e, kept, sent,
        after=parts[:1],
        alias=[(9, 2), (10, 3)],
    )
    first_set = GradSum(kept, sent, FIRST_PHASES[0]() + FIRST_PHASES[1]())
    first_scattered = first_set.scatter(0, after=parts[1:])
    total_5, upr, same_s, edge_s, sums = call(
        bound(kernel_6),
        [small(2 * step), plane(narrow), like(same, BF16), like(edge, BF16), small(2 * step)],
        *parts, mask8, total_1, total_2, ups, zs, zr, spatial_norm, reduce_norm, spatial_weight,
        lists=len(parts),
        after=[first_scattered],
    )
    parts = clip_parts(sums)
    upr_sums = sums
    spare = 128
    set_rows = 9 * half + wide // 2 + spare
    kept, sent = call(
        kernel_spatial,
        [like((set_rows, 256), BF16)] * 2,
        ra, same_s, edge_s,
        after=parts[:1],
    )
    last = kept
    for k in range(1, EARLY + 1):
        last = first_set.scatter(k, after=[last])
    back_r, kept, sent = call(
        kernel_7,
        [plane(narrow, BF16)] + [like((set_rows, 256), BF16)] * 2,
        *parts, mask8, total_1, upr, zr, reduce_norm, x, upr_sums, ups_sums, up1_sums, up2_sums, kept, sent,
        lists=len(parts),
        after=[last],
        alias=[(len(parts) + 10, 1), (len(parts) + 11, 2)],
    )
    second_set = GradSum(kept, sent, SECOND_PHASES[0]() + SECOND_PHASES[1]())

    taps = like((9, narrow, narrow), F32)
    made = {}

    def iframe(after):
        made["iframe"], token = call(
            kernel_iframe, [like(gx.shape, BF16)], mask8, gx, upe, back_r, reduce_weight,
            after=after, token=True,
        )
        return token

    def motion(after):
        made["motion"], token = call(
            kernel_motion, [like(gm.shape, BF16)], mask8, same_1, edge_1, motion_first, gm, up2,
            after=after, token=True,
        )
        return token

    def outputs(after):
        *made["outputs"], token = call(
            bound(kernel_out),
            [like(gx.shape, BF16), like(gm.shape, BF16)],
            mask8, total_1, total_2, total_3, ze, x, z2, m, expand_norm, second_norm,
            after=after, token=True,
        )
        return token

    def finish(after):
        *made["first"], token = first_set.finish(
            ("taps", "taps", "wide"), [taps, taps, like(expand_weight.shape, F32)], token=True
        )
        return token

    last = kept
    for step in ORDER:
        if step == "I":
            last = iframe([last])
        elif step == "M":
            last = motion([last])
        elif step == "O":
            last = outputs([last])
        elif step == "X":
            last = finish([last])
        else:
            own = first_set if step[0] == "F" else second_set
            after = [last] if len(step) < 4 else []
            if step[1] == "t":
                last = own.total(after)
            elif step[1] == "s":
                last = own.scatter(int(step[2]), after)
            else:
                last = own.gather(int(step[2]), after)
    iframe_back, motion_back = made["iframe"], made["motion"]
    iframe_out, motion_out = made["outputs"]
    grad_second, grad_first, grad_expand = made["first"]
    norms = (reduce_norm, spatial_norm, expand_norm, first_norm, second_norm)
    starts = [0]
    for norm in norms:
        starts.append(starts[-1] + norm.size // 256)
    grad_spatial, grad_reduce, *norm_grads = second_set.finish(
        ["taps", "taps"] + starts[:-1],
        [taps, like((1, wide, narrow), F32)] + [like(norm.shape, F32) for norm in norms],
    )
    features = tuple(frames_first(v) for v in (iframe_out, motion_out, iframe_back, motion_back))
    return features + (
        grad_reduce[0],
        grad_spatial.reshape(spatial_weight.shape),
        grad_expand,
        grad_first.reshape(motion_first.shape),
        grad_second.reshape(motion_second.shape),
    ) + tuple(norm_grads)


def solution(mesh):
    shared = (P("section", "clip", None, None, None),) * 4
    return jax.shard_map(
        per_device,
        mesh=mesh,
        in_specs=shared + (P(None, "clip"),) + (P(),) * 10,
        out_specs=shared + (P(),) * 10,
        check_vma=False,
    )
```

```python
import functools

import jax
import jax.numpy as jnp
from jax import lax
from jax.experimental import pallas as pl
from jax.experimental.pallas import tpu as pltpu
from jax.sharding import PartitionSpec as P

EPS = 1e-05
LANES = 128
COST = 1024
F32 = jnp.float32
BF16 = jnp.bfloat16


def factors(size):
    steps = []
    stride = 1
    if size % 2 == 0:
        steps.append((stride, 2))
        stride, size = 2, size // 2
    while size % 4 == 0:
        steps.append((stride, 4))
        stride, size = stride * 4, size // 4
    while size % 2 == 0:
        steps.append((stride, 2))
        stride, size = stride * 2, size // 2
    return steps, size


def swap(value, axis, mask):
    size = lax.axis_size(axis)
    return lax.ppermute(value, axis, [(i, i ^ mask) for i in range(size)])


def clip_parts(value):
    steps, rest = factors(lax.axis_size("clip"))
    if rest != 1:
        return [lax.psum(value, "clip")]
    for stride, radix in steps[:-1]:
        parts = [swap(value, "clip", stride * k) for k in range(1, radix)]
        for part in parts:
            value = value + part
    stride, radix = steps[-1]
    return [value] + [swap(value, "clip", stride * k) for k in range(1, radix)]


def silu_of_half(v):
    return v * (1.0 + jnp.tanh(v))


def twice_slope_of_half(v):
    t = jnp.tanh(v)
    return (1.0 + t) * (1.0 + v * (1.0 - t))


def total_of(refs):
    total = refs[0][...]
    for ref in refs[1:]:
        total = total + ref[...]
    return total


def row_of(total, row, channels):
    count = channels // LANES
    return jnp.concatenate([total[row + k : row + k + 1] for k in range(count)], axis=1)


def put_row(ref, row, value):
    for k in range(value.shape[1] // LANES):
        ref[row + k : row + k + 1, :] = value[:, k * LANES : (k + 1) * LANES]


def moments(total, row, apart, channels, count):
    mean = row_of(total, row, channels) / count
    square = row_of(total, row + apart, channels) / count
    return mean, lax.rsqrt(square - mean * mean + EPS)


def eights(value):
    return value.reshape(-1, 8, value.shape[-1])


def rows_of(value):
    return value.reshape(-1, value.shape[-1])


def down(value):
    return jnp.sum(jnp.sum(value, axis=0), axis=0, keepdims=True)


def spread(value, width, frames, same_ref, edge_ref):
    rows, channels = value.shape
    line = width * frames
    index = lax.broadcasted_iota(jnp.int32, (line, channels), 0)
    first = jnp.where(index < frames, 0.0, 1.0).astype(F32)
    final = jnp.where(index >= line - frames, 0.0, 1.0).astype(F32)
    before = pltpu.roll(value, frames, 0).reshape(-1, line, channels) * first
    after = pltpu.roll(value, rows - frames, 0).reshape(-1, line, channels) * final
    zeros = jnp.zeros((line, channels), F32)
    for k, part in enumerate((rows_of(before), value, rows_of(after))):
        lanes = slice(k * channels, (k + 1) * channels)
        same_ref[:, lanes] = part.astype(BF16)
        edge_ref[:, lanes] = jnp.concatenate([zeros, part, zeros], axis=0).astype(BF16)


def tap_rows(same_ref, edge_ref, a):
    rows = same_ref.shape[0]
    if a == 1:
        return same_ref[...]
    start = a * (edge_ref.shape[0] - rows) // 2
    return edge_ref[start : start + rows, :]


def conv_of(same_ref, edge_ref, kernel_ref):
    total = None
    for a in range(3):
        matrix = kernel_ref[a].reshape(-1, kernel_ref.shape[3])
        part = jnp.dot(tap_rows(same_ref, edge_ref, a), matrix, preferred_element_type=F32)
        total = part if total is None else total + part
    return total


def conv_back_of(same_ref, edge_ref, kernel_ref):
    total = None
    channels = kernel_ref.shape[3]
    for a in range(3):
        rows = tap_rows(same_ref, edge_ref, a)
        for b in range(3):
            part = lax.dot_general(
                rows[:, b * channels : (b + 1) * channels],
                kernel_ref[2 - a, 2 - b],
                (((1,), (1,)), ((), ())),
                preferred_element_type=F32,
            )
            total = part if total is None else total + part
    return total


def split_store(core, keep_ref, send_ref, row, value):
    half = value.shape[0] // 2
    low, high = value[:half].astype(BF16), value[half:].astype(BF16)
    keep_ref[row : row + half, :] = jnp.where(core == 0, low, high)
    send_ref[row : row + half, :] = jnp.where(core == 0, high, low)


def across(first, second):
    return lax.dot_general(first, second, (((0,), (0,)), ((), ())), preferred_element_type=F32)


def conv_grad_to(core, picture, same_ref, edge_ref, keep_ref, send_ref, row):
    channels = same_ref.shape[1] // 3
    half = picture.shape[1] // 2
    for a in range(3):
        product = across(picture, tap_rows(same_ref, edge_ref, a))
        for b in range(3):
            tap = 3 * (2 - a) + 2 - b
            part = product[:, b * channels : (b + 1) * channels]
            split_store(core, keep_ref, send_ref, row + tap * half, part)


def back_of(up, z, mean, scale, gain, total_up, total_cross, count, mask):
    share = total_cross * scale / count
    start = total_up / count - mean * share
    return rows_of((gain * scale) * (eights(up) - mask * (start + eights(z) * share)))


def slope_back(grad, z, mean, scale, norm, ups_ref):
    gain = 0.5 * norm[0:1] * scale
    half = z * gain + (0.5 * norm[1:2] - mean * gain)
    up = (0.5 * grad.astype(BF16).astype(F32)) * twice_slope_of_half(half)
    ups_ref[...] = up
    total_up = down(eights(up))
    return total_up, scale * (down(eights(up * z)) - mean * total_up)


def kernel_1(width, valid_far, x_far, m_far, reduce_far, first_far, mask8, zr, z1, sums, *rest):
    same, edge, valid, x, m, reduce_w, first_w, arrived = rest
    copies = []
    for k, (far, near) in enumerate(
        ((m_far, m), (valid_far, valid), (first_far, first_w), (x_far, x), (reduce_far, reduce_w))
    ):
        copies.append(pltpu.make_async_copy(far, near, arrived.at[k]))
        copies[k].start()
    channels = z1.shape[1]
    frames = m.shape[1]
    copies[0].wait()
    spread(rows_of(m[...]).astype(F32), width, frames, same, edge)
    copies[1].wait()
    section = lax.axis_index("section")
    keep = [valid[section, f].astype(F32) for f in range(frames)]
    frame = lax.rem(lax.broadcasted_iota(jnp.int32, (8, channels), 0), frames)
    mask = jnp.full((8, channels), 0.0, F32)
    for f in range(frames):
        mask = jnp.where(frame == f, keep[f], mask)
    mask8[...] = mask
    copies[2].wait()
    z1[...] = conv_of(same, edge, first_w)
    copies[3].wait()
    copies[4].wait()
    zr[...] = jnp.dot(rows_of(x[...]), reduce_w[...], preferred_element_type=F32)
    step = channels // LANES
    sums[...] = jnp.zeros(sums.shape, F32)
    for k, ref in enumerate((zr, z1)):
        z = eights(ref[...])
        kept = mask * z
        put_row(sums, 2 * k * step, down(kept))
        put_row(sums, (2 * k + 1) * step, down(kept * z))
    put_row(sums, 4 * step, jnp.full((1, LANES), 1.0, F32) * (sum(keep) * x.shape[0]))


def kernel_2(place, parts, mask8, zr, z1, reduce_n, first_n, spatial_w, second_w, *rest):
    total_1, ra, mm, zs, z2, sums, same, edge = rest
    channels = zr.shape[1]
    step = channels // LANES
    total = total_of(parts)
    total_1[...] = total
    count = total[4 * step : 4 * step + 1, 0:1]
    mask = mask8[...]
    for k, (z_ref, norm, act, weight, out) in enumerate(
        ((zr, reduce_n, ra, spatial_w, zs), (z1, first_n, mm, second_w, z2))
    ):
        mean, scale = moments(total, 2 * k * step, step, channels, count)
        gain = 0.5 * norm[0:1] * scale
        value = silu_of_half(z_ref[...] * gain + (0.5 * norm[1:2] - mean * gain))
        act[...] = value.astype(BF16)
        spread(value, *place, same, edge)
        out[...] = conv_of(same, edge, weight)
        z = eights(out[...])
        kept = mask * z
        put_row(sums, 2 * k * step, down(kept))
        put_row(sums, (2 * k + 1) * step, down(kept * z))


def kernel_3(parts, mask8, total_1, zs, z2, m, gm, spatial_n, second_n, expand_w, *rest):
    total_2, sa, ze, up2, sums = rest
    channels, wide = zs.shape[1], ze.shape[1]
    step, wide_step = channels // LANES, wide // LANES
    total = total_of(parts)
    total_2[...] = total
    count = total_1[4 * step : 4 * step + 1, 0:1]
    mean, scale = moments(total, 0, step, channels, count)
    gain = 0.5 * spatial_n[0:1] * scale
    sa[...] = silu_of_half(zs[...] * gain + (0.5 * spatial_n[1:2] - mean * gain)).astype(BF16)
    mask = mask8[...]
    sums[...] = jnp.zeros(sums.shape, F32)
    for at in range(0, wide, channels):
        lanes = slice(at, at + channels)
        ze[:, lanes] = jnp.dot(sa[...], expand_w[:, lanes], preferred_element_type=F32)
        z = eights(ze[:, lanes])
        kept = z * mask
        put_row(sums, at // LANES, down(kept))
        put_row(sums, wide_step + at // LANES, down(kept * z))
    mean, scale = moments(total, 2 * step, step, channels, count)
    gain = 0.5 * second_n[0:1] * scale
    z = eights(z2[...])
    half = z * gain + (0.5 * second_n[1:2] - mean * gain) + 0.5 * eights(rows_of(m[...]).astype(F32))
    up = (eights(rows_of(gm[...]).astype(F32)) * (0.5 * mask)) * twice_slope_of_half(half)
    up2[...] = rows_of(up)
    total_up = down(up)
    put_row(sums, 2 * wide_step, total_up)
    put_row(sums, 2 * wide_step + step, scale * (down(up * z) - mean * total_up))


def kernel_4(place, parts, mask8, total_1, total_2, z1, z2, up2, ze, x, gx, *rest):
    expand_n, second_n, first_n, second_w = rest[:4]
    total_3, upe, up1, same, edge, sums = rest[4:]
    channels, wide = z1.shape[1], ze.shape[1]
    step, wide_step = channels // LANES, wide // LANES
    total = total_of(parts)
    total_3[...] = total
    count = total_1[4 * step : 4 * step + 1, 0:1]
    mask = mask8[...]

    mean, scale = moments(total_2[...], 2 * step, step, channels, count)
    low = back_of(
        up2[...], z2[...], mean, scale, second_n[0:1], row_of(total, 2 * wide_step, channels),
        row_of(total, 2 * wide_step + step, channels), count, mask,
    )
    spread(low.astype(BF16).astype(F32), *place, same, edge)
    mid_grad = conv_back_of(same, edge, second_w)
    mean, scale = moments(total_1[...], 2 * step, step, channels, count)
    total_up, total_cross = slope_back(mid_grad, z1[...], mean, scale, first_n, up1)
    sums[...] = jnp.zeros(sums.shape, F32)
    put_row(sums, 2 * wide_step, total_up)
    put_row(sums, 2 * wide_step + step, total_cross)

    part, rows = channels, 16
    frames = place[1]
    eight = (8, part)
    half_mask = 0.5 * mask
    for at in range(0, wide, part):
        lanes = slice(at, at + part)
        mean, scale = moments(total, at // LANES, wide_step, part, count)
        gain = 0.5 * expand_n[0:1, lanes] * scale
        gain8 = jnp.broadcast_to(gain, eight)
        shift8 = jnp.broadcast_to(0.5 * expand_n[1:2, lanes] - mean * gain, eight)

        def step_of(i, totals):
            here = pl.ds(pl.multiple_of(i * rows, rows), rows)
            pixels = pl.ds(i * (rows // frames), rows // frames)
            z = eights(ze[here, lanes])
            x_here = eights(rows_of(x[pixels, :, lanes]).astype(F32))
            g_here = eights(rows_of(gx[pixels, :, lanes]).astype(F32))
            half = z * gain8 + shift8 + 0.5 * x_here
            up = (g_here * half_mask) * twice_slope_of_half(half)
            upe[here, lanes] = rows_of(up)
            return (totals[0] + jnp.sum(up, axis=0), totals[1] + jnp.sum(up * z, axis=0))

        empty = (jnp.zeros(eight, F32), jnp.zeros(eight, F32))
        totals = lax.fori_loop(0, ze.shape[0] // rows, step_of, empty, unroll=True)
        total_up = down(totals[0][None])
        put_row(sums, at // LANES, total_up)
        total_cross = scale * (down(totals[1][None]) - mean * total_up)
        put_row(sums, wide_step + at // LANES, total_cross)


def kernel_5(parts, mask8, total_1, total_2, total_3, ze, upe, zs, expand_n, spatial_n, expand_w, *rest):
    total_4, back_e, ups, sums = rest
    channels, wide = zs.shape[1], ze.shape[1]
    step, wide_step = channels // LANES, wide // LANES
    total = total_of(parts)
    total_4[...] = total
    count = total_1[4 * step : 4 * step + 1, 0:1]
    mask = mask8[...]
    grad = None
    for at in range(0, wide, channels):
        lanes = slice(at, at + channels)
        mean, scale = moments(total_3[...], at // LANES, wide_step, channels, count)
        low = back_of(
            upe[:, lanes], ze[:, lanes], mean, scale, expand_n[0:1, lanes],
            row_of(total, at // LANES, channels), row_of(total, wide_step + at // LANES, channels),
            count, mask,
        )
        back_e[:, lanes] = low.astype(BF16)
        part = lax.dot_general(
            back_e[:, lanes], expand_w[:, lanes], (((1,), (1,)), ((), ())), preferred_element_type=F32
        )
        grad = part if grad is None else grad + part
    mean, scale = moments(total_2[...], 0, step, channels, count)
    total_up, total_cross = slope_back(grad, zs[...], mean, scale, spatial_n, ups)
    sums[...] = jnp.zeros(sums.shape, F32)
    put_row(sums, 0, total_up)
    put_row(sums, step, total_cross)


def kernel_6(place, parts, mask8, total_1, total_2, ups, zs, zr, spatial_n, reduce_n, spatial_w, *rest):
    total_5, upr, same, edge, sums = rest
    channels = zs.shape[1]
    step = channels // LANES
    total = total_of(parts)
    total_5[...] = total
    count = total_1[4 * step : 4 * step + 1, 0:1]
    mask = mask8[...]
    mean, scale = moments(total_2[...], 0, step, channels, count)
    low = back_of(
        ups[...], zs[...], mean, scale, spatial_n[0:1], row_of(total, 0, channels),
        row_of(total, step, channels), count, mask,
    )
    spread(low.astype(BF16).astype(F32), *place, same, edge)
    grad = conv_back_of(same, edge, spatial_w)
    mean, scale = moments(total_1[...], 0, step, channels, count)
    total_up, total_cross = slope_back(grad, zr[...], mean, scale, reduce_n, upr)
    sums[...] = jnp.zeros(sums.shape, F32)
    put_row(sums, 0, total_up)
    put_row(sums, step, total_cross)


def kernel_second(mm, same, edge, kept_ref, sent_ref):
    conv_grad_to(core_here(), mm[...], same, edge, kept_ref, sent_ref, 0)


def kernel_first(place, mask8, total_1, total_4, up1, z1, first_n, m, sa, back_e, *rest):
    kept_in, sent_in, same, edge, kept_ref, sent_ref = rest
    channels = z1.shape[1]
    step, wide_step = channels // LANES, back_e.shape[1] // LANES
    count = total_1[4 * step : 4 * step + 1, 0:1]
    mean, scale = moments(total_1[...], 2 * step, step, channels, count)
    total = total_4[...]
    low = back_of(
        up1[...], z1[...], mean, scale, first_n[0:1], row_of(total, 2 * wide_step, channels),
        row_of(total, 2 * wide_step + step, channels), count, mask8[...],
    )
    spread(low.astype(BF16).astype(F32), *place, same, edge)
    core = core_here()
    half = channels // 2
    conv_grad_to(core, rows_of(m[...]), same, edge, kept_ref, sent_ref, 9 * half)
    for k in range(back_e.shape[1] // 256):
        product = across(sa[...], back_e[:, k * 256 : (k + 1) * 256])
        split_store(core, kept_ref, sent_ref, (18 + k) * half, product)


def kernel_motion(mask8, same, edge, first_w, gm, up2, motion_back):
    out = conv_back_of(same, edge, first_w) + up2[...]
    out = rows_of(eights(out) + eights(rows_of(gm[...]).astype(F32)) * (1.0 - mask8[...]))
    motion_back[...] = out.astype(BF16).reshape(motion_back.shape)


def kernel_spatial(ra, same, edge, kept_ref, sent_ref):
    conv_grad_to(core_here(), ra[...], same, edge, kept_ref, sent_ref, 0)


def kernel_7(parts, mask8, total_1, upr, zr, reduce_n, x, sums_r, sums_s, sums_1, sums_2, *rest):
    kept_in, sent_in, back_r, kept_ref, sent_ref = rest
    channels, wide = zr.shape[1], x.shape[2]
    step = channels // LANES
    total = total_of(parts)
    count = total_1[4 * step : 4 * step + 1, 0:1]
    mean, scale = moments(total_1[...], 0, step, channels, count)
    low = back_of(
        upr[...], zr[...], mean, scale, reduce_n[0:1], row_of(total, 0, channels),
        row_of(total, step, channels), count, mask8[...],
    )
    back_r[...] = low.astype(BF16)
    core = core_here()
    at = 9 * (channels // 2)
    split_store(core, kept_ref, sent_ref, at, across(rows_of(x[...]), back_r[...]))
    at = at + wide // 2
    rows = norm_rows(sums_r, 0, channels) + norm_rows(sums_s, 0, channels)
    rows += norm_rows(sums_1, 0, wide) + norm_rows(sums_1, 2 * wide // LANES, channels)
    rows += norm_rows(sums_2, 2 * wide // LANES, channels)
    half = kept_ref.shape[0] - at
    rows.append(jnp.zeros((2 * half - len(rows), 256), F32))
    split_store(core, kept_ref, sent_ref, at, jnp.concatenate(rows, axis=0))


def kernel_out(place, mask8, total_1, total_2, total_3, ze, x, z2, m, expand_n, second_n, iframe_out, motion_out):
    channels, wide = z2.shape[1], ze.shape[1]
    step, wide_step = channels // LANES, wide // LANES
    count = total_1[4 * step : 4 * step + 1, 0:1]
    mask = mask8[...]

    def folded(mean, scale, norm):
        gain = 0.5 * norm[0:1] * scale
        shape = (8, gain.shape[1])
        return jnp.broadcast_to(gain, shape), jnp.broadcast_to(0.5 * norm[1:2] - mean * gain, shape)

    def joined(z, here, gain, shift):
        out = silu_of_half(eights(z) * gain + shift + 0.5 * here)
        return rows_of(here + mask * (out - here)).astype(BF16)

    mean, scale = moments(total_2[...], 2 * step, step, channels, count)
    gain, shift = folded(mean, scale, second_n[...])
    motion = eights(rows_of(m[...]).astype(F32))
    motion_out[...] = joined(z2[...], motion, gain, shift).reshape(motion_out.shape)
    part, rows, frames = channels, 16, place[1]
    for at in range(0, wide, part):
        lanes = slice(at, at + part)
        mean, scale = moments(total_3[...], at // LANES, wide_step, part, count)
        gain, shift = folded(mean, scale, expand_n[:, lanes])

        def step_of(i, carry):
            here = pl.ds(pl.multiple_of(i * rows, rows), rows)
            pixels = pl.ds(i * (rows // frames), rows // frames)
            frame = eights(rows_of(x[pixels, :, lanes]).astype(F32))
            out = joined(ze[here, lanes], frame, gain, shift)
            iframe_out[pixels, :, lanes] = out.reshape(-1, frames, part)
            return carry

        lax.fori_loop(0, ze.shape[0] // rows, step_of, 0, unroll=True)


def norm_rows(sums, row, channels):
    count = channels // LANES
    starts = list(range(row + count, row + 2 * count, 2)) + list(range(row, row + count, 2))
    return [jnp.concatenate([sums[k : k + 1, :], sums[k + 1 : k + 2, :]], axis=1) for k in starts]


def kernel_iframe(mask8, gx, upe, back_r, reduce_w, iframe_back):
    wide, part = upe.shape[1], 256
    mask, frames = mask8[...], gx.shape[1]
    for at in range(0, wide, part):
        lanes = slice(at, at + part)
        out = upe[:, lanes] + lax.dot_general(
            back_r[...], reduce_w[lanes, :], (((1,), (1,)), ((), ())), preferred_element_type=F32
        )
        out = eights(out) + eights(rows_of(gx[:, :, lanes]).astype(F32)) * (1.0 - mask)
        iframe_back[:, :, lanes] = rows_of(out).astype(BF16).reshape(-1, frames, part)


def core_here():
    return lax.rem(lax.axis_index("clip"), 2)


def kernel_scatter(phase, *refs):
    here, radix = phase.digit(), phase.radix
    ins, outs = refs[:-radix], refs[-radix:]
    for k in range(radix):
        at = jnp.bitwise_xor(here, k)
        total = ins[0][at].astype(F32)
        for ref in ins[1:]:
            total = total + ref[at].astype(F32)
        outs[k][...] = total.astype(BF16)


def kernel_sum(*refs):
    total = refs[0][...].astype(F32)
    for ref in refs[1:-1]:
        total = total + ref[...].astype(F32)
    refs[-1][...] = total.astype(BF16)


def kernel_gather(phase, *refs):
    here = phase.digit()
    for k in range(phase.radix):
        refs[-1][jnp.bitwise_xor(here, k)] = refs[k][...]


def kernel_finish(kinds, own, other, *outs):
    core = core_here()
    at = 0

    def halves(ref, lanes, size, at):
        here = pl.ds(pl.multiple_of(core * size, size), size)
        there = pl.ds(pl.multiple_of((1 - core) * size, size), size)
        ref[here, lanes] = own[at : at + size, :].astype(F32)
        ref[there, lanes] = other[at : at + size, :].astype(F32)

    for kind, out in zip(kinds, outs):
        if kind == "taps":
            size = out.shape[1] // 2
            for k in range(out.shape[0]):
                halves(out.at[k], slice(None), size, at)
                at = at + size
        elif kind == "wide":
            size = out.shape[0] // 2
            for k in range(out.shape[1] // 256):
                halves(out, slice(k * 256, (k + 1) * 256), size, at)
                at = at + size
        else:
            mine, his = own[at : at + 16, :].astype(F32), other[at : at + 16, :].astype(F32)
            rows = jnp.where(core == 0, mine, his)
            start = kind
            count = out.shape[1] // 256
            for k in range(2):
                for j in range(count):
                    row = start + k * count + j
                    out[k : k + 1, j * 256 : (j + 1) * 256] = rows[row : row + 1]


def call(kernel, outs, *args, scratch=(), lists=None, space=pltpu.VMEM, after=(), alias=(), token=False):
    used = len(args)
    if token:
        outs = list(outs) + [like((8, LANES), F32)]

    def body(*refs):
        refs = refs[:used] + refs[used + len(after) :]
        if token:
            at = used + len(outs) - 1
            refs[at][...] = jnp.zeros((8, LANES), F32)
            refs = refs[:at] + refs[at + 1 :]
        if lists:
            return kernel(refs[:lists], *refs[lists:])
        return kernel(*refs)

    return pl.pallas_call(
        body,
        out_shape=outs,
        in_specs=[pl.BlockSpec(memory_space=space) for _ in args]
        + [pl.BlockSpec(memory_space=pl.ANY) for _ in after],
        out_specs=[pl.BlockSpec(memory_space=pltpu.VMEM) for _ in outs],
        scratch_shapes=list(scratch),
        input_output_aliases=dict(alias),
        compiler_params=pltpu.CompilerParams(vmem_limit_bytes=20 << 20),
        cost_estimate=pl.CostEstimate(flops=COST, bytes_accessed=COST, transcendentals=0),
    )(*args, *after)


def like(shape, dtype):
    return jax.ShapeDtypeStruct(shape, dtype)


class Phase:
    def __init__(self, radix, digit, partner):
        self.radix, self.digit, self.partner = radix, digit, partner

    def send(self, value, k):
        sections, clips = lax.axis_size("section"), lax.axis_size("clip")
        route = []
        for s in range(sections):
            for c in range(clips):
                to, where = self.partner(s, c, k)
                route.append((s * clips + c, to * clips + where))
        return lax.ppermute(value, ("section", "clip"), route)


def over_section():
    size = lax.axis_size("section")
    return [Phase(size, lambda: lax.axis_index("section"), lambda s, c, k: (s ^ k, c))]


def over_section_halves():
    if lax.axis_size("section") != 4:
        return over_section()

    def digit(swapped):
        section = lax.axis_index("section")
        first = jnp.bitwise_xor(core_here(), swapped) == 0
        return jnp.where(first, lax.rem(section, 2), section // 2)

    def partner(swapped, s, c, k):
        return s ^ (k if (c % 2) ^ swapped == 0 else 2 * k), c

    return [
        Phase(2, functools.partial(digit, swapped), functools.partial(partner, swapped))
        for swapped in (0, 1)
    ]


def over_clip():
    def phase(stride, radix):
        return Phase(
            radix,
            lambda: lax.rem(lax.axis_index("clip") // stride, radix),
            lambda s, c, k: (s, c ^ (stride * k)),
        )

    return [phase(stride, radix) for stride, radix in factors(lax.axis_size("clip"))[0][1:]]


def over_clip_halves():
    def digit(stride, swapped):
        first = jnp.bitwise_xor(core_here(), swapped) == 0
        place = lax.axis_index("clip") // stride
        return jnp.where(first, lax.rem(place, 2), lax.rem(place // 2, 2))

    def partner(stride, swapped, s, c, k):
        return s, c ^ (stride * (k if (c % 2) ^ swapped == 0 else 2 * k))

    phases = []
    for step, (stride, radix) in zip(over_clip(), factors(lax.axis_size("clip"))[0][1:]):
        if radix != 4:
            phases.append(step)
            continue
        for swapped in (0, 1):
            phases.append(
                Phase(
                    2,
                    functools.partial(digit, stride, swapped),
                    functools.partial(partner, stride, swapped),
                )
            )
    return phases


class GradSum:
    def __init__(self, kept, sent, phases):
        self.phases = phases
        self.rows, self.width = kept.shape
        self.parts = [kept, swap(sent, "clip", 1)]

    def scatter(self, k, after=()):
        phase = self.phases[k]
        radix = phase.radix
        self.rows = self.rows // radix
        chunks = call(
            functools.partial(kernel_scatter, phase),
            [like((self.rows, self.width), BF16)] * radix,
            *[part.reshape(radix, self.rows, self.width) for part in self.parts],
            after=after,
        )
        self.parts = [chunks[0]] + [phase.send(chunks[j], j) for j in range(1, radix)]
        return chunks[0]

    def spread_from(self, value, k):
        phase = self.phases[k]
        self.parts = [value] + [phase.send(value, j) for j in range(1, phase.radix)]
        return value

    def total(self, after=()):
        (value,) = call(kernel_sum, [like((self.rows, self.width), BF16)], *self.parts, after=after)
        return self.spread_from(value, len(self.phases) - 1)

    def gather(self, k, after=()):
        radix = self.phases[k].radix
        (value,) = call(
            functools.partial(kernel_gather, self.phases[k]),
            [like((radix, self.rows, self.width), BF16)],
            *self.parts,
            after=after,
        )
        self.rows = radix * self.rows
        value = value.reshape(self.rows, self.width)
        if k:
            return self.spread_from(value, k - 1)
        self.parts = [value, swap(value, "clip", 1)]
        return value

    def finish(self, kinds, outs, token=False):
        return call(functools.partial(kernel_finish, kinds), outs, *self.parts, token=token)


FIRST_PHASES = (over_section_halves, over_clip)
SECOND_PHASES = (over_section, over_clip)
EARLY = 1
ORDER = ('Ts0', 'I', 'M', 'Fs2', 'Ts1', 'Ft', 'Fg2', 'Tt', 'Fg1', 'O', 'Tg1', 'Fg0', 'X', 'Tg0')


def per_device(
    iframe_act,
    motion_act,
    iframe_grad,
    motion_grad,
    segment_valid,
    reduce_weight,
    spatial_weight,
    expand_weight,
    motion_first,
    motion_second,
    reduce_norm,
    spatial_norm,
    expand_norm,
    first_norm,
    second_norm,
):
    frames, height, width, wide = iframe_act.shape[1:]
    narrow = motion_act.shape[4]

    def pixels_first(value):
        return jnp.transpose(value[0], (1, 2, 0, 3)).reshape(height * width, frames, value.shape[4])

    def frames_first(value):
        value = value.reshape(height, width, frames, value.shape[2])
        return jnp.transpose(value, (2, 0, 1, 3))[None]

    x, m, gx, gm = [pixels_first(v) for v in (iframe_act, motion_act, iframe_grad, motion_grad)]
    step, wide_step = narrow // LANES, wide // LANES
    area = height * width * frames

    def plane(channels, dtype=F32):
        return like((area, channels), dtype)

    def small(count):
        return like(((count + 7) // 8 * 8, LANES), F32)

    def bound(kernel):
        return functools.partial(kernel, (width, frames))

    def far(value):
        return pltpu.with_memory_space_constraint(value, pltpu.HBM)

    same = (area, 3 * narrow)
    edge = (area + 2 * width * frames, 3 * narrow)
    spread_scratch = [pltpu.VMEM(same, BF16), pltpu.VMEM(edge, BF16)]
    first_size, second_size = small(4 * step + 1), small(4 * step)
    both = small(2 * wide_step + 2 * step)

    mask8, zr, z1, sums = call(
        functools.partial(kernel_1, width),
        [like((8, narrow), F32), plane(narrow), plane(narrow), first_size],
        *[far(v) for v in (segment_valid, x, m, reduce_weight, motion_first)],
        scratch=spread_scratch
        + [pltpu.SMEM(segment_valid.shape, jnp.int32)]
        + [pltpu.VMEM(v.shape, BF16) for v in (x, m, reduce_weight, motion_first)]
        + [pltpu.SemaphoreType.DMA((5,))],
        space=pltpu.HBM,
    )
    parts = clip_parts(sums)
    total_1, ra, mm, zs, z2, sums = call(
        bound(kernel_2),
        [first_size, plane(narrow, BF16), plane(narrow, BF16), plane(narrow), plane(narrow), second_size],
        *parts, mask8, zr, z1, reduce_norm, first_norm, spatial_weight, motion_second,
        scratch=spread_scratch,
        lists=len(parts),
    )
    parts = clip_parts(sums)
    total_2, sa, ze, up2, sums = call(
        kernel_3,
        [second_size, plane(narrow, BF16), plane(wide), plane(narrow), both],
        *parts, mask8, total_1, zs, z2, m, gm, spatial_norm, second_norm, expand_weight,
        lists=len(parts),
    )
    parts = clip_parts(sums)
    up2_sums = sums
    total_3, upe, up1, same_2, edge_2, sums = call(
        bound(kernel_4),
        [both, plane(wide), plane(narrow), like(same, BF16), like(edge, BF16), both],
        *parts, mask8, total_1, total_2, z1, z2, up2, ze, x, gx,
        expand_norm, second_norm, first_norm, motion_second,
        lists=len(parts),
    )
    parts = clip_parts(sums)
    up1_sums = sums
    half = narrow // 2
    set_rows = (18 + wide // 256) * half
    kept, sent = call(
        kernel_second,
        [like((set_rows, 256), BF16)] * 2,
        mm, same_2, edge_2,
        after=parts[:1],
    )
    total_4, back_e, ups, sums = call(
        kernel_5,
        [both, plane(wide, BF16), plane(narrow), small(2 * step)],
        *parts, mask8, total_1, total_2, total_3, ze, upe, zs, expand_norm, spatial_norm, expand_weight,
        lists=len(parts),
        after=[kept],
    )
    parts = clip_parts(sums)
    ups_sums = sums
    same_1, edge_1, kept, sent = call(
        bound(kernel_first),
        [like(same, BF16), like(edge, BF16)] + [like((set_rows, 256), BF16)] * 2,
        mask8, total_1, total_4, up1, z1, first_norm, m, sa, back_e, kept, sent,
        after=parts[:1],
        alias=[(9, 2), (10, 3)],
    )
    first_set = GradSum(kept, sent, FIRST_PHASES[0]() + FIRST_PHASES[1]())
    first_scattered = first_set.scatter(0, after=parts[1:])
    total_5, upr, same_s, edge_s, sums = call(
        bound(kernel_6),
        [small(2 * step), plane(narrow), like(same, BF16), like(edge, BF16), small(2 * step)],
        *parts, mask8, total_1, total_2, ups, zs, zr, spatial_norm, reduce_norm, spatial_weight,
        lists=len(parts),
        after=[first_scattered],
    )
    parts = clip_parts(sums)
    upr_sums = sums
    spare = 128
    set_rows = 9 * half + wide // 2 + spare
    kept, sent = call(
        kernel_spatial,
        [like((set_rows, 256), BF16)] * 2,
        ra, same_s, edge_s,
        after=parts[:1],
    )
    last = kept
    for k in range(1, EARLY + 1):
        last = first_set.scatter(k, after=[last])
    back_r, kept, sent = call(
        kernel_7,
        [plane(narrow, BF16)] + [like((set_rows, 256), BF16)] * 2,
        *parts, mask8, total_1, upr, zr, reduce_norm, x, upr_sums, ups_sums, up1_sums, up2_sums, kept, sent,
        lists=len(parts),
        after=[last],
        alias=[(len(parts) + 10, 1), (len(parts) + 11, 2)],
    )
    second_set = GradSum(kept, sent, SECOND_PHASES[0]() + SECOND_PHASES[1]())

    taps = like((9, narrow, narrow), F32)
    made = {}

    def iframe(after):
        made["iframe"], token = call(
            kernel_iframe, [like(gx.shape, BF16)], mask8, gx, upe, back_r, reduce_weight,
            after=after, token=True,
        )
        return token

    def motion(after):
        made["motion"], token = call(
            kernel_motion, [like(gm.shape, BF16)], mask8, same_1, edge_1, motion_first, gm, up2,
            after=after, token=True,
        )
        return token

    def outputs(after):
        *made["outputs"], token = call(
            bound(kernel_out),
            [like(gx.shape, BF16), like(gm.shape, BF16)],
            mask8, total_1, total_2, total_3, ze, x, z2, m, expand_norm, second_norm,
            after=after, token=True,
        )
        return token

    def finish(after):
        *made["first"], token = first_set.finish(
            ("taps", "taps", "wide"), [taps, taps, like(expand_weight.shape, F32)], token=True
        )
        return token

    last = kept
    for step in ORDER:
        if step == "I":
            last = iframe([last])
        elif step == "M":
            last = motion([last])
        elif step == "O":
            last = outputs([last])
        elif step == "X":
            last = finish([last])
        else:
            own = first_set if step[0] == "F" else second_set
            after = [last] if len(step) < 4 else []
            if step[1] == "t":
                last = own.total(after)
            elif step[1] == "s":
                last = own.scatter(int(step[2]), after)
            else:
                last = own.gather(int(step[2]), after)
    iframe_back, motion_back = made["iframe"], made["motion"]
    iframe_out, motion_out = made["outputs"]
    grad_second, grad_first, grad_expand = made["first"]
    norms = (reduce_norm, spatial_norm, expand_norm, first_norm, second_norm)
    starts = [0]
    for norm in norms:
        starts.append(starts[-1] + norm.size // 256)
    grad_spatial, grad_reduce, *norm_grads = second_set.finish(
        ["taps", "taps"] + starts[:-1],
        [taps, like((1, wide, narrow), F32)] + [like(norm.shape, F32) for norm in norms],
    )
    features = tuple(frames_first(v) for v in (iframe_out, motion_out, iframe_back, motion_back))
    return features + (
        grad_reduce[0],
        grad_spatial.reshape(spatial_weight.shape),
        grad_expand,
        grad_first.reshape(motion_first.shape),
        grad_second.reshape(motion_second.shape),
    ) + tuple(norm_grads)


def solution(mesh):
    shared = (P("section", "clip", None, None, None),) * 4
    return jax.shard_map(
        per_device,
        mesh=mesh,
        in_specs=shared + (P(None, "clip"),) + (P(),) * 10,
        out_specs=shared + (P(),) * 10,
        check_vma=False,
    )
```

```python
import functools

import jax
import jax.numpy as jnp
from jax import lax
from jax.experimental import pallas as pl
from jax.experimental.pallas import tpu as pltpu
from jax.sharding import PartitionSpec as P

EPS = 1e-05
LANES = 128
COST = 1024
F32 = jnp.float32
BF16 = jnp.bfloat16


def factors(size):
    steps = []
    stride = 1
    if size % 2 == 0:
        steps.append((stride, 2))
        stride, size = 2, size // 2
    while size % 4 == 0:
        steps.append((stride, 4))
        stride, size = stride * 4, size // 4
    while size % 2 == 0:
        steps.append((stride, 2))
        stride, size = stride * 2, size // 2
    return steps, size


def swap(value, axis, mask):
    size = lax.axis_size(axis)
    return lax.ppermute(value, axis, [(i, i ^ mask) for i in range(size)])


def clip_parts(value):
    steps, rest = factors(lax.axis_size("clip"))
    if rest != 1:
        return [lax.psum(value, "clip")]
    for stride, radix in steps[:-1]:
        parts = [swap(value, "clip", stride * k) for k in range(1, radix)]
        for part in parts:
            value = value + part
    stride, radix = steps[-1]
    return [value] + [swap(value, "clip", stride * k) for k in range(1, radix)]


def silu_of_half(v):
    return v * (1.0 + jnp.tanh(v))


def twice_slope_of_half(v):
    t = jnp.tanh(v)
    return (1.0 + t) * (1.0 + v * (1.0 - t))


def total_of(refs):
    total = refs[0][...]
    for ref in refs[1:]:
        total = total + ref[...]
    return total


def row_of(total, row, channels):
    count = channels // LANES
    return jnp.concatenate([total[row + k : row + k + 1] for k in range(count)], axis=1)


def put_row(ref, row, value):
    for k in range(value.shape[1] // LANES):
        ref[row + k : row + k + 1, :] = value[:, k * LANES : (k + 1) * LANES]


def moments(total, row, apart, channels, count):
    mean = row_of(total, row, channels) / count
    square = row_of(total, row + apart, channels) / count
    return mean, lax.rsqrt(square - mean * mean + EPS)


def eights(value):
    return value.reshape(-1, 8, value.shape[-1])


def rows_of(value):
    return value.reshape(-1, value.shape[-1])


def down(value):
    return jnp.sum(jnp.sum(value, axis=0), axis=0, keepdims=True)


def spread(value, width, frames, same_ref, edge_ref):
    rows, channels = value.shape
    line = width * frames
    index = lax.broadcasted_iota(jnp.int32, (line, channels), 0)
    first = jnp.where(index < frames, 0.0, 1.0).astype(F32)
    final = jnp.where(index >= line - frames, 0.0, 1.0).astype(F32)
    before = pltpu.roll(value, frames, 0).reshape(-1, line, channels) * first
    after = pltpu.roll(value, rows - frames, 0).reshape(-1, line, channels) * final
    zeros = jnp.zeros((line, channels), F32)
    for k, part in enumerate((rows_of(before), value, rows_of(after))):
        lanes = slice(k * channels, (k + 1) * channels)
        same_ref[:, lanes] = part.astype(BF16)
        edge_ref[:, lanes] = jnp.concatenate([zeros, part, zeros], axis=0).astype(BF16)


def tap_rows(same_ref, edge_ref, a):
    rows = same_ref.shape[0]
    if a == 1:
        return same_ref[...]
    start = a * (edge_ref.shape[0] - rows) // 2
    return edge_ref[start : start + rows, :]


def conv_of(same_ref, edge_ref, kernel_ref):
    total = None
    for a in range(3):
        matrix = kernel_ref[a].reshape(-1, kernel_ref.shape[3])
        part = jnp.dot(tap_rows(same_ref, edge_ref, a), matrix, preferred_element_type=F32)
        total = part if total is None else total + part
    return total


def conv_back_of(same_ref, edge_ref, kernel_ref):
    total = None
    channels = kernel_ref.shape[3]
    for a in range(3):
        rows = tap_rows(same_ref, edge_ref, a)
        for b in range(3):
            part = lax.dot_general(
                rows[:, b * channels : (b + 1) * channels],
                kernel_ref[2 - a, 2 - b],
                (((1,), (1,)), ((), ())),
                preferred_element_type=F32,
            )
            total = part if total is None else total + part
    return total


def split_store(core, keep_ref, send_ref, row, value):
    half = value.shape[0] // 2
    low, high = value[:half].astype(BF16), value[half:].astype(BF16)
    keep_ref[row : row + half, :] = jnp.where(core == 0, low, high)
    send_ref[row : row + half, :] = jnp.where(core == 0, high, low)


def across(first, second):
    return lax.dot_general(first, second, (((0,), (0,)), ((), ())), preferred_element_type=F32)


def conv_grad_to(core, picture, same_ref, edge_ref, keep_ref, send_ref, row):
    channels = same_ref.shape[1] // 3
    half = picture.shape[1] // 2
    for a in range(3):
        product = across(picture, tap_rows(same_ref, edge_ref, a))
        for b in range(3):
            tap = 3 * (2 - a) + 2 - b
            part = product[:, b * channels : (b + 1) * channels]
            split_store(core, keep_ref, send_ref, row + tap * half, part)


def back_of(up, z, mean, scale, gain, total_up, total_cross, count, mask):
    share = total_cross * scale / count
    start = total_up / count - mean * share
    return rows_of((gain * scale) * (eights(up) - mask * (start + eights(z) * share)))


def slope_back(grad, z, mean, scale, norm, ups_ref):
    gain = 0.5 * norm[0:1] * scale
    half = z * gain + (0.5 * norm[1:2] - mean * gain)
    up = (0.5 * grad.astype(BF16).astype(F32)) * twice_slope_of_half(half)
    ups_ref[...] = up
    total_up = down(eights(up))
    return total_up, scale * (down(eights(up * z)) - mean * total_up)


def kernel_1(width, valid_far, x_far, m_far, reduce_far, first_far, mask8, zr, z1, sums, *rest):
    same, edge, valid, x, m, reduce_w, first_w, arrived = rest
    copies = []
    for k, (far, near) in enumerate(
        ((m_far, m), (valid_far, valid), (first_far, first_w), (x_far, x), (reduce_far, reduce_w))
    ):
        copies.append(pltpu.make_async_copy(far, near, arrived.at[k]))
        copies[k].start()
    channels = z1.shape[1]
    frames = m.shape[1]
    copies[0].wait()
    spread(rows_of(m[...]).astype(F32), width, frames, same, edge)
    copies[1].wait()
    section = lax.axis_index("section")
    keep = [valid[section, f].astype(F32) for f in range(frames)]
    frame = lax.rem(lax.broadcasted_iota(jnp.int32, (8, channels), 0), frames)
    mask = jnp.full((8, channels), 0.0, F32)
    for f in range(frames):
        mask = jnp.where(frame == f, keep[f], mask)
    mask8[...] = mask
    copies[2].wait()
    z1[...] = conv_of(same, edge, first_w)
    copies[3].wait()
    copies[4].wait()
    zr[...] = jnp.dot(rows_of(x[...]), reduce_w[...], preferred_element_type=F32)
    step = channels // LANES
    sums[...] = jnp.zeros(sums.shape, F32)
    for k, ref in enumerate((zr, z1)):
        z = eights(ref[...])
        kept = mask * z
        put_row(sums, 2 * k * step, down(kept))
        put_row(sums, (2 * k + 1) * step, down(kept * z))
    put_row(sums, 4 * step, jnp.full((1, LANES), 1.0, F32) * (sum(keep) * x.shape[0]))


def kernel_2(place, parts, mask8, zr, z1, reduce_n, first_n, spatial_w, second_w, *rest):
    total_1, ra, mm, zs, z2, sums, same, edge = rest
    channels = zr.shape[1]
    step = channels // LANES
    total = total_of(parts)
    total_1[...] = total
    count = total[4 * step : 4 * step + 1, 0:1]
    mask = mask8[...]
    for k, (z_ref, norm, act, weight, out) in enumerate(
        ((zr, reduce_n, ra, spatial_w, zs), (z1, first_n, mm, second_w, z2))
    ):
        mean, scale = moments(total, 2 * k * step, step, channels, count)
        gain = 0.5 * norm[0:1] * scale
        value = silu_of_half(z_ref[...] * gain + (0.5 * norm[1:2] - mean * gain))
        act[...] = value.astype(BF16)
        spread(value, *place, same, edge)
        out[...] = conv_of(same, edge, weight)
        z = eights(out[...])
        kept = mask * z
        put_row(sums, 2 * k * step, down(kept))
        put_row(sums, (2 * k + 1) * step, down(kept * z))


def kernel_3(parts, mask8, total_1, zs, z2, m, gm, spatial_n, second_n, expand_w, *rest):
    total_2, sa, ze, up2, sums = rest
    channels, wide = zs.shape[1], ze.shape[1]
    step, wide_step = channels // LANES, wide // LANES
    total = total_of(parts)
    total_2[...] = total
    count = total_1[4 * step : 4 * step + 1, 0:1]
    mean, scale = moments(total, 0, step, channels, count)
    gain = 0.5 * spatial_n[0:1] * scale
    sa[...] = silu_of_half(zs[...] * gain + (0.5 * spatial_n[1:2] - mean * gain)).astype(BF16)
    mask = mask8[...]
    sums[...] = jnp.zeros(sums.shape, F32)
    for at in range(0, wide, channels):
        lanes = slice(at, at + channels)
        ze[:, lanes] = jnp.dot(sa[...], expand_w[:, lanes], preferred_element_type=F32)
        z = eights(ze[:, lanes])
        kept = z * mask
        put_row(sums, at // LANES, down(kept))
        put_row(sums, wide_step + at // LANES, down(kept * z))
    mean, scale = moments(total, 2 * step, step, channels, count)
    gain = 0.5 * second_n[0:1] * scale
    z = eights(z2[...])
    half = z * gain + (0.5 * second_n[1:2] - mean * gain) + 0.5 * eights(rows_of(m[...]).astype(F32))
    up = (eights(rows_of(gm[...]).astype(F32)) * (0.5 * mask)) * twice_slope_of_half(half)
    up2[...] = rows_of(up)
    total_up = down(up)
    put_row(sums, 2 * wide_step, total_up)
    put_row(sums, 2 * wide_step + step, scale * (down(up * z) - mean * total_up))


def kernel_4(place, parts, mask8, total_1, total_2, z1, z2, up2, ze, x, gx, *rest):
    expand_n, second_n, first_n, second_w = rest[:4]
    total_3, upe, up1, same, edge, sums = rest[4:]
    channels, wide = z1.shape[1], ze.shape[1]
    step, wide_step = channels // LANES, wide // LANES
    total = total_of(parts)
    total_3[...] = total
    count = total_1[4 * step : 4 * step + 1, 0:1]
    mask = mask8[...]

    mean, scale = moments(total_2[...], 2 * step, step, channels, count)
    low = back_of(
        up2[...], z2[...], mean, scale, second_n[0:1], row_of(total, 2 * wide_step, channels),
        row_of(total, 2 * wide_step + step, channels), count, mask,
    )
    spread(low.astype(BF16).astype(F32), *place, same, edge)
    mid_grad = conv_back_of(same, edge, second_w)
    mean, scale = moments(total_1[...], 2 * step, step, channels, count)
    total_up, total_cross = slope_back(mid_grad, z1[...], mean, scale, first_n, up1)
    sums[...] = jnp.zeros(sums.shape, F32)
    put_row(sums, 2 * wide_step, total_up)
    put_row(sums, 2 * wide_step + step, total_cross)

    part, rows = channels, 16
    frames = place[1]
    eight = (8, part)
    half_mask = 0.5 * mask
    for at in range(0, wide, part):
        lanes = slice(at, at + part)
        mean, scale = moments(total, at // LANES, wide_step, part, count)
        gain = 0.5 * expand_n[0:1, lanes] * scale
        gain8 = jnp.broadcast_to(gain, eight)
        shift8 = jnp.broadcast_to(0.5 * expand_n[1:2, lanes] - mean * gain, eight)

        def step_of(i, totals):
            here = pl.ds(pl.multiple_of(i * rows, rows), rows)
            pixels = pl.ds(i * (rows // frames), rows // frames)
            z = eights(ze[here, lanes])
            x_here = eights(rows_of(x[pixels, :, lanes]).astype(F32))
            g_here = eights(rows_of(gx[pixels, :, lanes]).astype(F32))
            half = z * gain8 + shift8 + 0.5 * x_here
            up = (g_here * half_mask) * twice_slope_of_half(half)
            upe[here, lanes] = rows_of(up)
            return (totals[0] + jnp.sum(up, axis=0), totals[1] + jnp.sum(up * z, axis=0))

        empty = (jnp.zeros(eight, F32), jnp.zeros(eight, F32))
        totals = lax.fori_loop(0, ze.shape[0] // rows, step_of, empty, unroll=True)
        total_up = down(totals[0][None])
        put_row(sums, at // LANES, total_up)
        total_cross = scale * (down(totals[1][None]) - mean * total_up)
        put_row(sums, wide_step + at // LANES, total_cross)


def kernel_5(parts, mask8, total_1, total_2, total_3, ze, upe, zs, expand_n, spatial_n, expand_w, *rest):
    total_4, back_e, ups, sums = rest
    channels, wide = zs.shape[1], ze.shape[1]
    step, wide_step = channels // LANES, wide // LANES
    total = total_of(parts)
    total_4[...] = total
    count = total_1[4 * step : 4 * step + 1, 0:1]
    mask = mask8[...]
    grad = None
    for at in range(0, wide, channels):
        lanes = slice(at, at + channels)
        mean, scale = moments(total_3[...], at // LANES, wide_step, channels, count)
        low = back_of(
            upe[:, lanes], ze[:, lanes], mean, scale, expand_n[0:1, lanes],
            row_of(total, at // LANES, channels), row_of(total, wide_step + at // LANES, channels),
            count, mask,
        )
        back_e[:, lanes] = low.astype(BF16)
        part = lax.dot_general(
            back_e[:, lanes], expand_w[:, lanes], (((1,), (1,)), ((), ())), preferred_element_type=F32
        )
        grad = part if grad is None else grad + part
    mean, scale = moments(total_2[...], 0, step, channels, count)
    total_up, total_cross = slope_back(grad, zs[...], mean, scale, spatial_n, ups)
    sums[...] = jnp.zeros(sums.shape, F32)
    put_row(sums, 0, total_up)
    put_row(sums, step, total_cross)


def kernel_6(place, parts, mask8, total_1, total_2, ups, zs, zr, spatial_n, reduce_n, spatial_w, *rest):
    total_5, upr, same, edge, sums = rest
    channels = zs.shape[1]
    step = channels // LANES
    total = total_of(parts)
    total_5[...] = total
    count = total_1[4 * step : 4 * step + 1, 0:1]
    mask = mask8[...]
    mean, scale = moments(total_2[...], 0, step, channels, count)
    low = back_of(
        ups[...], zs[...], mean, scale, spatial_n[0:1], row_of(total, 0, channels),
        row_of(total, step, channels), count, mask,
    )
    spread(low.astype(BF16).astype(F32), *place, same, edge)
    grad = conv_back_of(same, edge, spatial_w)
    mean, scale = moments(total_1[...], 0, step, channels, count)
    total_up, total_cross = slope_back(grad, zr[...], mean, scale, reduce_n, upr)
    sums[...] = jnp.zeros(sums.shape, F32)
    put_row(sums, 0, total_up)
    put_row(sums, step, total_cross)


def kernel_second(mm, same, edge, kept_ref, sent_ref):
    conv_grad_to(core_here(), mm[...], same, edge, kept_ref, sent_ref, 0)


def kernel_first(place, mask8, total_1, total_4, up1, z1, first_n, m, sa, back_e, *rest):
    kept_in, sent_in, same, edge, kept_ref, sent_ref = rest
    channels = z1.shape[1]
    step, wide_step = channels // LANES, back_e.shape[1] // LANES
    count = total_1[4 * step : 4 * step + 1, 0:1]
    mean, scale = moments(total_1[...], 2 * step, step, channels, count)
    total = total_4[...]
    low = back_of(
        up1[...], z1[...], mean, scale, first_n[0:1], row_of(total, 2 * wide_step, channels),
        row_of(total, 2 * wide_step + step, channels), count, mask8[...],
    )
    spread(low.astype(BF16).astype(F32), *place, same, edge)
    core = core_here()
    half = channels // 2
    conv_grad_to(core, rows_of(m[...]), same, edge, kept_ref, sent_ref, 9 * half)
    for k in range(back_e.shape[1] // 256):
        product = across(sa[...], back_e[:, k * 256 : (k + 1) * 256])
        split_store(core, kept_ref, sent_ref, (18 + k) * half, product)


def kernel_motion(mask8, same, edge, first_w, gm, up2, motion_back):
    out = conv_back_of(same, edge, first_w) + up2[...]
    out = rows_of(eights(out) + eights(rows_of(gm[...]).astype(F32)) * (1.0 - mask8[...]))
    motion_back[...] = out.astype(BF16).reshape(motion_back.shape)


def kernel_spatial(ra, same, edge, kept_ref, sent_ref):
    conv_grad_to(core_here(), ra[...], same, edge, kept_ref, sent_ref, 0)


def kernel_7(parts, mask8, total_1, upr, zr, reduce_n, x, sums_r, sums_s, sums_1, sums_2, *rest):
    kept_in, sent_in, back_r, kept_ref, sent_ref = rest
    channels, wide = zr.shape[1], x.shape[2]
    step = channels // LANES
    total = total_of(parts)
    count = total_1[4 * step : 4 * step + 1, 0:1]
    mean, scale = moments(total_1[...], 0, step, channels, count)
    low = back_of(
        upr[...], zr[...], mean, scale, reduce_n[0:1], row_of(total, 0, channels),
        row_of(total, step, channels), count, mask8[...],
    )
    back_r[...] = low.astype(BF16)
    core = core_here()
    at = 9 * (channels // 2)
    split_store(core, kept_ref, sent_ref, at, across(rows_of(x[...]), back_r[...]))
    at = at + wide // 2
    rows = norm_rows(sums_r, 0, channels) + norm_rows(sums_s, 0, channels)
    rows += norm_rows(sums_1, 0, wide) + norm_rows(sums_1, 2 * wide // LANES, channels)
    rows += norm_rows(sums_2, 2 * wide // LANES, channels)
    half = kept_ref.shape[0] - at
    rows.append(jnp.zeros((2 * half - len(rows), 256), F32))
    split_store(core, kept_ref, sent_ref, at, jnp.concatenate(rows, axis=0))


def kernel_out(place, mask8, total_1, total_2, total_3, ze, x, z2, m, expand_n, second_n, iframe_out, motion_out):
    channels, wide = z2.shape[1], ze.shape[1]
    step, wide_step = channels // LANES, wide // LANES
    count = total_1[4 * step : 4 * step + 1, 0:1]
    mask = mask8[...]

    def folded(mean, scale, norm):
        gain = 0.5 * norm[0:1] * scale
        shape = (8, gain.shape[1])
        return jnp.broadcast_to(gain, shape), jnp.broadcast_to(0.5 * norm[1:2] - mean * gain, shape)

    def joined(z, here, gain, shift):
        out = silu_of_half(eights(z) * gain + shift + 0.5 * here)
        return rows_of(here + mask * (out - here)).astype(BF16)

    mean, scale = moments(total_2[...], 2 * step, step, channels, count)
    gain, shift = folded(mean, scale, second_n[...])
    motion = eights(rows_of(m[...]).astype(F32))
    motion_out[...] = joined(z2[...], motion, gain, shift).reshape(motion_out.shape)
    part, rows, frames = channels, 16, place[1]
    for at in range(0, wide, part):
        lanes = slice(at, at + part)
        mean, scale = moments(total_3[...], at // LANES, wide_step, part, count)
        gain, shift = folded(mean, scale, expand_n[:, lanes])

        def step_of(i, carry):
            here = pl.ds(pl.multiple_of(i * rows, rows), rows)
            pixels = pl.ds(i * (rows // frames), rows // frames)
            frame = eights(rows_of(x[pixels, :, lanes]).astype(F32))
            out = joined(ze[here, lanes], frame, gain, shift)
            iframe_out[pixels, :, lanes] = out.reshape(-1, frames, part)
            return carry

        lax.fori_loop(0, ze.shape[0] // rows, step_of, 0, unroll=True)


def norm_rows(sums, row, channels):
    count = channels // LANES
    starts = list(range(row + count, row + 2 * count, 2)) + list(range(row, row + count, 2))
    return [jnp.concatenate([sums[k : k + 1, :], sums[k + 1 : k + 2, :]], axis=1) for k in starts]


def kernel_iframe(mask8, gx, upe, back_r, reduce_w, iframe_back):
    wide, part = upe.shape[1], 256
    mask, frames = mask8[...], gx.shape[1]
    for at in range(0, wide, part):
        lanes = slice(at, at + part)
        out = upe[:, lanes] + lax.dot_general(
            back_r[...], reduce_w[lanes, :], (((1,), (1,)), ((), ())), preferred_element_type=F32
        )
        out = eights(out) + eights(rows_of(gx[:, :, lanes]).astype(F32)) * (1.0 - mask)
        iframe_back[:, :, lanes] = rows_of(out).astype(BF16).reshape(-1, frames, part)


def core_here():
    return lax.rem(lax.axis_index("clip"), 2)


def kernel_scatter(phase, *refs):
    here, radix = phase.digit(), phase.radix
    ins, outs = refs[:-radix], refs[-radix:]
    for k in range(radix):
        at = jnp.bitwise_xor(here, k)
        total = ins[0][at].astype(F32)
        for ref in ins[1:]:
            total = total + ref[at].astype(F32)
        outs[k][...] = total.astype(BF16)


def kernel_sum(*refs):
    total = refs[0][...].astype(F32)
    for ref in refs[1:-1]:
        total = total + ref[...].astype(F32)
    refs[-1][...] = total.astype(BF16)


def kernel_gather(phase, *refs):
    here = phase.digit()
    for k in range(phase.radix):
        refs[-1][jnp.bitwise_xor(here, k)] = refs[k][...]


def kernel_finish(kinds, own, other, *outs):
    core = core_here()
    at = 0

    def halves(ref, lanes, size, at):
        here = pl.ds(pl.multiple_of(core * size, size), size)
        there = pl.ds(pl.multiple_of((1 - core) * size, size), size)
        ref[here, lanes] = own[at : at + size, :].astype(F32)
        ref[there, lanes] = other[at : at + size, :].astype(F32)

    for kind, out in zip(kinds, outs):
        if kind == "taps":
            size = out.shape[1] // 2
            for k in range(out.shape[0]):
                halves(out.at[k], slice(None), size, at)
                at = at + size
        elif kind == "wide":
            size = out.shape[0] // 2
            for k in range(out.shape[1] // 256):
                halves(out, slice(k * 256, (k + 1) * 256), size, at)
                at = at + size
        else:
            mine, his = own[at : at + 16, :].astype(F32), other[at : at + 16, :].astype(F32)
            rows = jnp.where(core == 0, mine, his)
            start = kind
            count = out.shape[1] // 256
            for k in range(2):
                for j in range(count):
                    row = start + k * count + j
                    out[k : k + 1, j * 256 : (j + 1) * 256] = rows[row : row + 1]


def call(kernel, outs, *args, scratch=(), lists=None, space=pltpu.VMEM, after=(), alias=(), token=False):
    used = len(args)
    if token:
        outs = list(outs) + [like((8, LANES), F32)]

    def body(*refs):
        refs = refs[:used] + refs[used + len(after) :]
        if token:
            at = used + len(outs) - 1
            refs[at][...] = jnp.zeros((8, LANES), F32)
            refs = refs[:at] + refs[at + 1 :]
        if lists:
            return kernel(refs[:lists], *refs[lists:])
        return kernel(*refs)

    return pl.pallas_call(
        body,
        out_shape=outs,
        in_specs=[pl.BlockSpec(memory_space=space) for _ in args]
        + [pl.BlockSpec(memory_space=pl.ANY) for _ in after],
        out_specs=[pl.BlockSpec(memory_space=pltpu.VMEM) for _ in outs],
        scratch_shapes=list(scratch),
        input_output_aliases=dict(alias),
        compiler_params=pltpu.CompilerParams(vmem_limit_bytes=20 << 20),
        cost_estimate=pl.CostEstimate(flops=COST, bytes_accessed=COST, transcendentals=0),
    )(*args, *after)


def like(shape, dtype):
    return jax.ShapeDtypeStruct(shape, dtype)


class Phase:
    def __init__(self, radix, digit, partner):
        self.radix, self.digit, self.partner = radix, digit, partner

    def send(self, value, k):
        sections, clips = lax.axis_size("section"), lax.axis_size("clip")
        route = []
        for s in range(sections):
            for c in range(clips):
                to, where = self.partner(s, c, k)
                route.append((s * clips + c, to * clips + where))
        return lax.ppermute(value, ("section", "clip"), route)


def over_section():
    size = lax.axis_size("section")
    return [Phase(size, lambda: lax.axis_index("section"), lambda s, c, k: (s ^ k, c))]


def over_section_halves():
    if lax.axis_size("section") != 4:
        return over_section()

    def digit(swapped):
        section = lax.axis_index("section")
        first = jnp.bitwise_xor(core_here(), swapped) == 0
        return jnp.where(first, lax.rem(section, 2), section // 2)

    def partner(swapped, s, c, k):
        return s ^ (k if (c % 2) ^ swapped == 0 else 2 * k), c

    return [
        Phase(2, functools.partial(digit, swapped), functools.partial(partner, swapped))
        for swapped in (0, 1)
    ]


def over_clip():
    def phase(stride, radix):
        return Phase(
            radix,
            lambda: lax.rem(lax.axis_index("clip") // stride, radix),
            lambda s, c, k: (s, c ^ (stride * k)),
        )

    return [phase(stride, radix) for stride, radix in factors(lax.axis_size("clip"))[0][1:]]


class GradSum:
    def __init__(self, kept, sent, phases):
        self.phases = phases
        self.rows, self.width = kept.shape
        self.parts = [kept, swap(sent, "clip", 1)]

    def scatter(self, k, after=()):
        phase = self.phases[k]
        radix = phase.radix
        self.rows = self.rows // radix
        chunks = call(
            functools.partial(kernel_scatter, phase),
            [like((self.rows, self.width), BF16)] * radix,
            *[part.reshape(radix, self.rows, self.width) for part in self.parts],
            after=after,
        )
        self.parts = [chunks[0]] + [phase.send(chunks[j], j) for j in range(1, radix)]
        return chunks[0]

    def spread_from(self, value, k):
        phase = self.phases[k]
        self.parts = [value] + [phase.send(value, j) for j in range(1, phase.radix)]
        return value

    def total(self, after=()):
        (value,) = call(kernel_sum, [like((self.rows, self.width), BF16)], *self.parts, after=after)
        return self.spread_from(value, len(self.phases) - 1)

    def gather(self, k, after=()):
        radix = self.phases[k].radix
        (value,) = call(
            functools.partial(kernel_gather, self.phases[k]),
            [like((radix, self.rows, self.width), BF16)],
            *self.parts,
            after=after,
        )
        self.rows = radix * self.rows
        value = value.reshape(self.rows, self.width)
        if k:
            return self.spread_from(value, k - 1)
        self.parts = [value, swap(value, "clip", 1)]
        return value

    def finish(self, kinds, outs, token=False):
        return call(functools.partial(kernel_finish, kinds), outs, *self.parts, token=token)


def order_of(early, clips):
    order = ["Ts0", "I", "M"]
    order += [f"Fs{early + k}" for k in range(clips)] + [f"Ts{1 + k}" for k in range(clips)]
    order += ["Ft"] + [f"Fg{early + k}" for k in reversed(range(clips))]
    order += ["Tt"] + [f"Tg{k}" for k in reversed(range(2, clips + 1))]
    order += [f"Fg{k}" for k in reversed(range(1, early))]
    return order + ["O", "Tg1", "Fg0", "X", "Tg0"]


def per_device(
    iframe_act,
    motion_act,
    iframe_grad,
    motion_grad,
    segment_valid,
    reduce_weight,
    spatial_weight,
    expand_weight,
    motion_first,
    motion_second,
    reduce_norm,
    spatial_norm,
    expand_norm,
    first_norm,
    second_norm,
):
    frames, height, width, wide = iframe_act.shape[1:]
    narrow = motion_act.shape[4]

    def pixels_first(value):
        return jnp.transpose(value[0], (1, 2, 0, 3)).reshape(height * width, frames, value.shape[4])

    def frames_first(value):
        value = value.reshape(height, width, frames, value.shape[2])
        return jnp.transpose(value, (2, 0, 1, 3))[None]

    x, m, gx, gm = [pixels_first(v) for v in (iframe_act, motion_act, iframe_grad, motion_grad)]
    step, wide_step = narrow // LANES, wide // LANES
    area = height * width * frames

    def plane(channels, dtype=F32):
        return like((area, channels), dtype)

    def small(count):
        return like(((count + 7) // 8 * 8, LANES), F32)

    def bound(kernel):
        return functools.partial(kernel, (width, frames))

    def far(value):
        return pltpu.with_memory_space_constraint(value, pltpu.HBM)

    same = (area, 3 * narrow)
    edge = (area + 2 * width * frames, 3 * narrow)
    spread_scratch = [pltpu.VMEM(same, BF16), pltpu.VMEM(edge, BF16)]
    first_size, second_size = small(4 * step + 1), small(4 * step)
    both = small(2 * wide_step + 2 * step)

    mask8, zr, z1, sums = call(
        functools.partial(kernel_1, width),
        [like((8, narrow), F32), plane(narrow), plane(narrow), first_size],
        *[far(v) for v in (segment_valid, x, m, reduce_weight, motion_first)],
        scratch=spread_scratch
        + [pltpu.SMEM(segment_valid.shape, jnp.int32)]
        + [pltpu.VMEM(v.shape, BF16) for v in (x, m, reduce_weight, motion_first)]
        + [pltpu.SemaphoreType.DMA((5,))],
        space=pltpu.HBM,
    )
    parts = clip_parts(sums)
    total_1, ra, mm, zs, z2, sums = call(
        bound(kernel_2),
        [first_size, plane(narrow, BF16), plane(narrow, BF16), plane(narrow), plane(narrow), second_size],
        *parts, mask8, zr, z1, reduce_norm, first_norm, spatial_weight, motion_second,
        scratch=spread_scratch,
        lists=len(parts),
    )
    parts = clip_parts(sums)
    total_2, sa, ze, up2, sums = call(
        kernel_3,
        [second_size, plane(narrow, BF16), plane(wide), plane(narrow), both],
        *parts, mask8, total_1, zs, z2, m, gm, spatial_norm, second_norm, expand_weight,
        lists=len(parts),
    )
    parts = clip_parts(sums)
    up2_sums = sums
    total_3, upe, up1, same_2, edge_2, sums = call(
        bound(kernel_4),
        [both, plane(wide), plane(narrow), like(same, BF16), like(edge, BF16), both],
        *parts, mask8, total_1, total_2, z1, z2, up2, ze, x, gx,
        expand_norm, second_norm, first_norm, motion_second,
        lists=len(parts),
    )
    parts = clip_parts(sums)
    up1_sums = sums
    half = narrow // 2
    set_rows = (18 + wide // 256) * half
    kept, sent = call(
        kernel_second,
        [like((set_rows, 256), BF16)] * 2,
        mm, same_2, edge_2,
        after=parts[:1],
    )
    total_4, back_e, ups, sums = call(
        kernel_5,
        [both, plane(wide, BF16), plane(narrow), small(2 * step)],
        *parts, mask8, total_1, total_2, total_3, ze, upe, zs, expand_norm, spatial_norm, expand_weight,
        lists=len(parts),
        after=[kept],
    )
    parts = clip_parts(sums)
    ups_sums = sums
    same_1, edge_1, kept, sent = call(
        bound(kernel_first),
        [like(same, BF16), like(edge, BF16)] + [like((set_rows, 256), BF16)] * 2,
        mask8, total_1, total_4, up1, z1, first_norm, m, sa, back_e, kept, sent,
        after=parts[:1],
        alias=[(9, 2), (10, 3)],
    )
    first_set = GradSum(kept, sent, over_section_halves() + over_clip())
    first_scattered = first_set.scatter(0, after=parts[1:])
    total_5, upr, same_s, edge_s, sums = call(
        bound(kernel_6),
        [small(2 * step), plane(narrow), like(same, BF16), like(edge, BF16), small(2 * step)],
        *parts, mask8, total_1, total_2, ups, zs, zr, spatial_norm, reduce_norm, spatial_weight,
        lists=len(parts),
        after=[first_scattered],
    )
    parts = clip_parts(sums)
    upr_sums = sums
    spare = 128
    set_rows = 9 * half + wide // 2 + spare
    kept, sent = call(
        kernel_spatial,
        [like((set_rows, 256), BF16)] * 2,
        ra, same_s, edge_s,
        after=parts[:1],
    )
    last = kept
    early = len(over_section_halves())
    for k in range(1, early):
        last = first_set.scatter(k, after=[last])
    back_r, kept, sent = call(
        kernel_7,
        [plane(narrow, BF16)] + [like((set_rows, 256), BF16)] * 2,
        *parts, mask8, total_1, upr, zr, reduce_norm, x, upr_sums, ups_sums, up1_sums, up2_sums, kept, sent,
        lists=len(parts),
        after=[last],
        alias=[(len(parts) + 10, 1), (len(parts) + 11, 2)],
    )
    second_set = GradSum(kept, sent, over_section() + over_clip())

    taps = like((9, narrow, narrow), F32)
    made = {}

    def iframe(after):
        made["iframe"], token = call(
            kernel_iframe, [like(gx.shape, BF16)], mask8, gx, upe, back_r, reduce_weight,
            after=after, token=True,
        )
        return token

    def motion(after):
        made["motion"], token = call(
            kernel_motion, [like(gm.shape, BF16)], mask8, same_1, edge_1, motion_first, gm, up2,
            after=after, token=True,
        )
        return token

    def outputs(after):
        *made["outputs"], token = call(
            bound(kernel_out),
            [like(gx.shape, BF16), like(gm.shape, BF16)],
            mask8, total_1, total_2, total_3, ze, x, z2, m, expand_norm, second_norm,
            after=after, token=True,
        )
        return token

    def finish(after):
        *made["first"], token = first_set.finish(
            ("taps", "taps", "wide"), [taps, taps, like(expand_weight.shape, F32)], token=True
        )
        return token

    last = kept
    for step in order_of(early, len(over_clip())):
        if step == "I":
            last = iframe([last])
        elif step == "M":
            last = motion([last])
        elif step == "O":
            last = outputs([last])
        elif step == "X":
            last = finish([last])
        else:
            own = first_set if step[0] == "F" else second_set
            if step[1] == "t":
                last = own.total([last])
            elif step[1] == "s":
                last = own.scatter(int(step[2:]), [last])
            else:
                last = own.gather(int(step[2:]), [last])
    iframe_back, motion_back = made["iframe"], made["motion"]
    iframe_out, motion_out = made["outputs"]
    grad_second, grad_first, grad_expand = made["first"]
    norms = (reduce_norm, spatial_norm, expand_norm, first_norm, second_norm)
    starts = [0]
    for norm in norms:
        starts.append(starts[-1] + norm.size // 256)
    grad_spatial, grad_reduce, *norm_grads = second_set.finish(
        ["taps", "taps"] + starts[:-1],
        [taps, like((1, wide, narrow), F32)] + [like(norm.shape, F32) for norm in norms],
    )
    features = tuple(frames_first(v) for v in (iframe_out, motion_out, iframe_back, motion_back))
    return features + (
        grad_reduce[0],
        grad_spatial.reshape(spatial_weight.shape),
        grad_expand,
        grad_first.reshape(motion_first.shape),
        grad_second.reshape(motion_second.shape),
    ) + tuple(norm_grads)


def solution(mesh):
    shared = (P("section", "clip", None, None, None),) * 4
    return jax.shard_map(
        per_device,
        mesh=mesh,
        in_specs=shared + (P(None, "clip"),) + (P(),) * 10,
        out_specs=shared + (P(),) * 10,
        check_vma=False,
    )
```
